512 devices in a mesh: col: 8 (over z_hi, core), row: 64 (over z_lo, y, x).
Axes of the slice: x: 4, y: 8, z: 8 (z_hi: 4, z_lo: 2; z = z_hi * 2 + z_lo), core: 2. Of those that a mesh axis runs over, the one named last changes fastest.
Arguments:
- matrix: float32 [16384, 4096], P('row', 'col'), may hold values from -100 to 100
- seats: int32 [16], replicated, may hold values from 0 to 15, each once
Outputs:
- rotated: float32 [16384, 4096], P('row', 'col')
- mean_squares: float32 [4096], P('col')
The draws below stay inside these ranges and needn't reach their ends.
All inputs are finite; a program needn't handle non-finite values.
Results may differ from the reference program's by a relative error of at most 0.0003.
Values sent between devices are 32-bit elements; how exact they have to be, the bound alone decides.
No kernel may reach another device: no remote copies, remote signals or barrier semaphores. Data moves between devices by JAX's collectives and lax.ppermute only.
A program may use at most 64 MiB of HBM per device.

```python
import math
import jax
import jax.numpy as jnp
from jax import lax

BLOCK = 256
ROWS = 16384
BLOCKS = 16
COLS = 4096
N_COL = 8


def draw_matrix(key, part):
    key = jax.random.fold_in(key, 11)
    keys = jax.random.split(key, 5)
    noise = jax.random.truncated_normal(keys[0], -4.0, 4.0, (ROWS, COLS), jnp.float32)
    shared = jax.random.truncated_normal(keys[1], -4.0, 4.0, (ROWS, BLOCK), jnp.float32)
    mix = jax.random.uniform(keys[2], (BLOCKS, 1), jnp.float32, 0.4, 1.0)
    mixed = noise.reshape(ROWS, BLOCKS, BLOCK) + mix[None, :, :] * shared[:, None, :]
    position = jnp.arange(ROWS, dtype=jnp.float32) / ROWS - 0.5
    trend = jnp.exp(math.log(3.0) * position)
    row_scale = trend * jnp.exp(jax.random.uniform(keys[3], (ROWS,), jnp.float32, math.log(0.5), math.log(2.0)))
    col_scale = jnp.exp(jax.random.uniform(keys[4], (COLS,), jnp.float32, math.log(0.35), math.log(3.5)))
    return (mixed.reshape(ROWS, COLS) * row_scale[:, None] * col_scale[None, :]).astype(jnp.float32)


def setup_inputs(seed: int = 0) -> dict:
    seeds = jax.random.split(jax.random.key(seed), 3)
    matrix = draw_matrix(jax.random.fold_in(seeds[2], 71), 0)
    seats = jax.random.permutation(seeds[1], BLOCKS).astype(jnp.int32)
    return {"matrix": matrix, "seats": seats}


HIGH = lax.Precision.HIGHEST

def mat(a, b):
    return jnp.dot(a, b, precision=HIGH, preferred_element_type=jnp.float32)

def root_poly(square):
    eye = jnp.eye(square.shape[0], dtype=jnp.float32)
    first = 1.5 * eye - 0.5 * square
    ystep = mat(square, first)
    second = 1.5 * eye - 0.5 * mat(first, ystep)
    return mat(second, first)

def pair_update(left, right):
    count = left.shape[0]
    cross = mat(left.T, right)
    mean_left = lax.optimization_barrier(jnp.sum(left * left, axis=0)) / count
    mean_right = lax.optimization_barrier(jnp.sum(right * right, axis=0)) / count
    coupling = 0.5 * (cross / count) / jnp.sqrt((mean_left[:, None] + 1e-06) * (mean_right[None, :] + 1e-06))
    eye = jnp.eye(coupling.shape[0], dtype=jnp.float32)
    zleft = root_poly(eye + mat(coupling, coupling.T))
    zright = root_poly(eye + mat(coupling.T, coupling))
    new_left = mat(left - mat(right, coupling.T), zleft)
    new_right = mat(right + mat(left, coupling), zright)
    return (new_left, new_right)

def reference(matrix, seats):
    pairs = N_COL
    tops = [matrix[:, 2 * c * BLOCK:(2 * c + 1) * BLOCK] for c in range(pairs)]
    bottoms = [matrix[:, (2 * c + 1) * BLOCK:(2 * c + 2) * BLOCK] for c in range(pairs)]
    for c in range(pairs):
        tops[c], bottoms[c] = pair_update(tops[c], bottoms[c])
    for i in range(pairs):
        other = (i + 2) % pairs
        tops[i], bottoms[other] = pair_update(tops[i], bottoms[other])
    pieces = []
    for c in range(pairs):
        pieces.append(tops[c])
        pieces.append(bottoms[c])
    rotated = jnp.concatenate(pieces, axis=1)
    squares = (lax.optimization_barrier(jnp.sum(rotated * rotated, axis=0)) / ROWS).reshape(BLOCKS, BLOCK)
    ordered = jnp.zeros((BLOCKS, BLOCK), jnp.float32).at[seats].set(squares)
    return (rotated, ordered.reshape(COLS))
```

```python
import jax
import jax.numpy as jnp
from jax import lax
from jax.sharding import PartitionSpec as P

PREC = lax.Precision.HIGH


def passed_along(block, axis, distance):
    devices = range(lax.axis_size(axis))
    route = [((i - distance) % len(devices), i) for i in devices]
    return lax.ppermute(block, axis, route)


def product(a, b, ca, cb):
    return lax.dot_general(
        a, b, (((ca,), (cb,)), ((), ())), precision=PREC, preferred_element_type=jnp.float32
    )


def exchange(pieces, axis):
    return lax.all_to_all(pieces, axis, 0, 0, tiled=True)


def root(s):
    eye = jnp.eye(s.shape[0], dtype=jnp.float32)
    s2 = product(s, s, 1, 0)
    return (eye - 0.5 * s + 0.375 * s2) + product(s2, 0.0625 * s2 - 0.3125 * s, 1, 0)


def couplings(left, right, total_rows):
    n = lax.axis_size("row")
    width = left.shape[1]
    cross = product(left, right, 0, 0)
    sum_left = jnp.sum(left * left, axis=0).reshape(2, 128)
    sum_right = jnp.sum(right * right, axis=0).reshape(2, 128)
    tiles = jnp.concatenate([cross[:, :128], cross[:, 128:]], axis=0).reshape(n, 1024)
    norm_left = jnp.tile(jnp.repeat(sum_left, n // 4, axis=0), (2, 1))
    norm_right = jnp.repeat(sum_right, n // 2, axis=0)
    payload = jnp.concatenate([tiles, norm_left, norm_right], axis=1)
    got = jnp.sum(exchange(payload.reshape(n, 1, 1280), "row"), axis=0).reshape(1280)
    tile = got[:1024].reshape(8, 128)
    start = 8 * (lax.axis_index("row") % 16)
    mean_left = lax.dynamic_slice(got[1024:1152], (start,), (8,)) / total_rows
    mean_right = got[1152:] / total_rows
    part = (
        0.5
        * (tile / total_rows)
        / jnp.sqrt((mean_left[:, None] + 1e-06) * (mean_right[None, :] + 1e-06))
    )
    whole = exchange(jnp.broadcast_to(part[None], (n, 8, 128)), "row").reshape(2 * width, 128)
    return jnp.concatenate([whole[:width], whole[width:]], axis=1)


def pair_update(left, right, total_rows):
    x = couplings(left, right, total_rows)
    new_left = product(
        left - product(right, x, 1, 1), root(product(x, x, 1, 1)), 1, 0
    )
    new_right = product(
        right + product(left, x, 1, 0), root(product(x, x, 0, 0)), 1, 0
    )
    return new_left, new_right


def on_device(matrix, seats):
    width = matrix.shape[1] // 2
    n, cols = lax.axis_size("row"), lax.axis_size("col")
    total_rows = matrix.shape[0] * n
    top = matrix[:, :width]
    bottom = matrix[:, width:]
    top, bottom = pair_update(top, bottom, total_rows)
    top = passed_along(top, "col", 1)
    bottom = passed_along(bottom, "col", -1)
    top, bottom = pair_update(top, bottom, total_rows)
    sums = jnp.concatenate([jnp.sum(top * top, axis=0), jnp.sum(bottom * bottom, axis=0)])
    top = passed_along(top, "col", -1)
    bottom = passed_along(bottom, "col", 1)
    final = jnp.concatenate([top, bottom], axis=1)
    sums = exchange(jnp.broadcast_to(sums.reshape(1, 4, 128), (n, 4, 128)), "row")
    means = jnp.sum(sums, axis=0) / total_rows
    table = exchange(jnp.broadcast_to(means[None], (cols, 4, 128)), "col")
    tops = jnp.roll(table[:, :2].reshape(cols, width), -1, axis=0)
    bottoms = jnp.roll(table[:, 2:].reshape(cols, width), 1, axis=0)
    by_seat = jnp.stack([tops, bottoms], axis=1).reshape(2 * cols, width)
    wanted = 2 * lax.axis_index("col") + jnp.arange(2, dtype=jnp.int32)
    hit = seats[None, :] == wanted[:, None]
    picked = jnp.sum(jnp.where(hit[:, :, None], by_seat[None], 0.0), axis=1)
    return (final, picked.reshape(2 * width))


def solution(mesh):
    placed = (P("row", "col"), P())
    return jax.shard_map(
        on_device,
        mesh=mesh,
        in_specs=placed,
        out_specs=(P("row", "col"), P("col")),
        check_vma=False,
    )
```

```python
import jax
import jax.numpy as jnp
from jax import lax
from jax.sharding import PartitionSpec as P

PREC = lax.Precision.HIGH


def swapped(block):
    cols = lax.axis_size("col")
    return lax.ppermute(
        block, "col", [(c, (c + (2 if c % 2 else -2)) % cols) for c in range(cols)]
    )


def swapped_back(block):
    cols = lax.axis_size("col")
    return lax.ppermute(
        block, "col", [(c, (c + (-2 if c % 2 else 2)) % cols) for c in range(cols)]
    )


def product(a, b, ca, cb):
    return lax.dot_general(
        a, b, (((ca,), (cb,)), ((), ())), precision=PREC, preferred_element_type=jnp.float32
    )


def exchange(pieces, axis):
    return lax.all_to_all(pieces, axis, 0, 0, tiled=True)


def root(s):
    eye = jnp.eye(s.shape[0], dtype=jnp.float32)
    s2 = product(s, s, 1, 0)
    return (eye - 0.5 * s + 0.375 * s2) + product(s2, 0.0625 * s2 - 0.3125 * s, 1, 0)


def couplings(left, right, sign, total_rows):
    n = lax.axis_size("row")
    width = left.shape[1]
    cross = product(left, right, 0, 0)
    sum_left = jnp.sum(left * left, axis=0).reshape(2, 128)
    sum_right = jnp.sum(right * right, axis=0).reshape(2, 128)
    tiles = jnp.concatenate([cross[:, :128], cross[:, 128:]], axis=0).reshape(n, 1024)
    norm_left = jnp.tile(jnp.repeat(sum_left, n // 4, axis=0), (2, 1))
    norm_right = jnp.repeat(sum_right, n // 2, axis=0)
    payload = jnp.concatenate([tiles, norm_left, norm_right], axis=1)
    got = jnp.sum(exchange(payload.reshape(n, 1, 1280), "row"), axis=0).reshape(1280)
    tile = got[:1024].reshape(8, 128)
    start = 8 * (lax.axis_index("row") % 16)
    mean_left = lax.dynamic_slice(got[1024:1152], (start,), (8,)) / total_rows
    mean_right = got[1152:] / total_rows
    part = (
        (0.5 * sign)
        * (tile / total_rows)
        / jnp.sqrt((mean_left[:, None] + 1e-06) * (mean_right[None, :] + 1e-06))
    )
    whole = exchange(jnp.broadcast_to(part[None], (n, 8, 128)), "row").reshape(2 * width, 128)
    return jnp.concatenate([whole[:width], whole[width:]], axis=1)


def pair_update(left, right, sign, total_rows):
    x = couplings(left, right, sign, total_rows)
    new_left = product(
        left - product(right, x, 1, 1), root(product(x, x, 1, 1)), 1, 0
    )
    new_right = product(
        right + product(left, x, 1, 0), root(product(x, x, 0, 0)), 1, 0
    )
    return new_left, new_right


def on_device(matrix, seats):
    width = matrix.shape[1] // 2
    n, cols = lax.axis_size("row"), lax.axis_size("col")
    total_rows = matrix.shape[0] * n
    odd = lax.axis_index("col") % 2 == 1
    keep = jnp.where(odd, matrix[:, width:], matrix[:, :width])
    move = jnp.where(odd, matrix[:, :width], matrix[:, width:])
    sign = jnp.where(odd, -1.0, 1.0).astype(jnp.float32)
    keep, move = pair_update(keep, move, sign, total_rows)
    keep, guest = pair_update(keep, swapped(move), sign, total_rows)
    sums = jnp.concatenate([jnp.sum(keep * keep, axis=0), jnp.sum(guest * guest, axis=0)])
    back = swapped_back(guest)
    final = jnp.concatenate(
        [jnp.where(odd, back, keep), jnp.where(odd, keep, back)], axis=1
    )
    sums = exchange(jnp.broadcast_to(sums.reshape(1, 4, 128), (n, 4, 128)), "row")
    means = jnp.sum(sums, axis=0) / total_rows
    table = exchange(jnp.broadcast_to(means[None], (cols, 4, 128)), "col")
    kept = table[:, :2].reshape(cols, width)
    guests = table[:, 2:].reshape(cols, width)
    rows = []
    for c in range(cols):
        rows.append(guests[(c + 2) % cols] if c % 2 else kept[c])
        rows.append(kept[c] if c % 2 else guests[(c - 2) % cols])
    by_seat = jnp.stack(rows)
    wanted = 2 * lax.axis_index("col") + jnp.arange(2, dtype=jnp.int32)
    hit = seats[None, :] == wanted[:, None]
    picked = jnp.sum(jnp.where(hit[:, :, None], by_seat[None], 0.0), axis=1)
    return (final, picked.reshape(2 * width))


def solution(mesh):
    placed = (P("row", "col"), P())
    return jax.shard_map(
        on_device,
        mesh=mesh,
        in_specs=placed,
        out_specs=(P("row", "col"), P("col")),
        check_vma=False,
    )
```

```python
import functools

import jax
import jax.numpy as jnp
from jax import lax
from jax.experimental import pallas as pl
from jax.experimental.pallas import tpu as pltpu
from jax.sharding import PartitionSpec as P

W = 256
N_ROW = 64
N_COL = 8
PIECE = 10
LIMIT = 32 * 1024 * 1024


def split(a):
    high = a.astype(jnp.bfloat16)
    return high, (a - high.astype(jnp.float32)).astype(jnp.bfloat16)


def product(a, b, ca=1, cb=0):
    def one(p, q):
        return lax.dot_general(
            p, q, (((ca,), (cb,)), ((), ())), preferred_element_type=jnp.float32
        )

    return one(a[0], b[0]) + (one(a[0], b[1]) + one(a[1], b[0]))


def root(s, also):
    parts = split(s)
    s2 = product(parts, parts)
    other = also()
    rows = lax.broadcasted_iota(jnp.int32, s.shape, 0)
    cols = lax.broadcasted_iota(jnp.int32, s.shape, 1)
    eye = jnp.where(rows == cols, 1.0, 0.0).astype(jnp.float32)
    base = eye - 0.5 * s + 0.375 * s2
    return base + product(split(s2), split(0.0625 * s2 - 0.3125 * s)), other


def kept_part(keep, guest, x):
    z, mixed = root(product(x, x, 1, 1), lambda: keep - product(split(guest), x, 1, 1))
    return product(split(mixed), split(z))


def guest_part(keep, guest, x):
    z, mixed = root(product(x, x, 0, 0), lambda: guest + product(split(keep), x))
    return product(split(mixed), split(z))


def coupling_of(tiles):
    return split(jnp.concatenate([tiles[:W], tiles[W:]], axis=1))


def pack(keep, guest, out):
    cross = product(split(keep), split(guest), 0, 0)
    norm_keep = jnp.sum(keep * keep, axis=0, keepdims=True)
    norm_guest = jnp.sum(guest * guest, axis=0, keepdims=True)
    for r in range(N_ROW):
        i, half = r % 32, r // 32
        at = PIECE * r
        out[at : at + 8, :] = cross[8 * i : 8 * i + 8, 128 * half : 128 * half + 128]
        out[at + 8 : at + 9, :] = norm_keep[:, 128 * (i // 16) : 128 * (i // 16) + 128]
        out[at + 9 : at + 10, :] = norm_guest[:, 128 * half : 128 * half + 128]


def halves(matrix):
    odd = lax.rem(lax.axis_index("col"), 2)
    keep = matrix[:, pl.ds(pl.multiple_of(odd * W, W), W)]
    move = matrix[:, pl.ds(pl.multiple_of((1 - odd) * W, W), W)]
    return keep, move


def pack_first(matrix, out):
    pack(*halves(matrix), out)


def pack_second(keep, guest, out):
    pack(keep[...], guest[...], out)


def fold(total_rows, got, out):
    tile = got[0:8, :]
    norms = got[8:10, :]
    for r in range(1, N_ROW):
        tile += got[PIECE * r : PIECE * r + 8, :]
        norms += got[PIECE * r + 8 : PIECE * r + 10, :]
    sign = jnp.where(lax.rem(lax.axis_index("col"), 2) == 1, -0.5, 0.5)
    first = 8 * lax.rem(lax.axis_index("row"), 16)
    lanes = lax.broadcasted_iota(jnp.int32, (8, 128), 1)
    rows = lax.broadcasted_iota(jnp.int32, (8, 128), 0)
    means = norms / total_rows
    mean_keep = jnp.sum(
        jnp.where(lanes == first + rows, means[0:1], 0.0), axis=1, keepdims=True
    )
    x = sign * (tile / total_rows) / jnp.sqrt((mean_keep + 1e-06) * (means[1:2] + 1e-06))
    for r in range(N_ROW):
        out[8 * r : 8 * r + 8, :] = x


def first_move(matrix, tiles, out):
    out[...] = guest_part(*halves(matrix), coupling_of(tiles[...]))


def first_keep(matrix, tiles, out):
    out[...] = kept_part(*halves(matrix), coupling_of(tiles[...]))


def second(keep, guest, tiles, new_keep, new_guest, sums):
    x = coupling_of(tiles[...])
    old_keep, old_guest = keep[...], guest[...]
    moved = guest_part(old_keep, old_guest, x)
    new_guest[...] = moved
    kept = kept_part(old_keep, old_guest, x)
    new_keep[...] = kept
    of_keep = jnp.sum(kept * kept, axis=0, keepdims=True)
    of_guest = jnp.sum(moved * moved, axis=0, keepdims=True)
    four = [of_keep[:, :128], of_keep[:, 128:], of_guest[:, :128], of_guest[:, 128:]]
    tile = jnp.concatenate(four + four, axis=0)
    for r in range(4 * N_ROW // 8):
        sums[8 * r : 8 * r + 8, :] = tile


def fold_sums(total_rows, got, out):
    tile = got[0:8, :]
    for r in range(1, 4 * N_ROW // 8):
        tile += got[8 * r : 8 * r + 8, :]
    four = (tile[0:4] + tile[4:8]) / total_rows
    tile = jnp.concatenate([four, four], axis=0)
    for r in range(4 * N_COL // 8):
        out[8 * r : 8 * r + 8, :] = tile


def local(body, flops, *shapes):
    out = [jax.ShapeDtypeStruct(shape, jnp.float32) for shape in shapes]

    def call(*args):
        moved = sum(4 * a.size for a in args) + sum(4 * s.size for s in out)
        return pl.pallas_call(
            body,
            out_shape=out if len(out) > 1 else out[0],
            in_specs=[pl.BlockSpec(memory_space=pltpu.VMEM)] * len(args),
            out_specs=[pl.BlockSpec(memory_space=pltpu.VMEM)] * len(out)
            if len(out) > 1
            else pl.BlockSpec(memory_space=pltpu.VMEM),
            cost_estimate=pl.CostEstimate(flops=flops, bytes_accessed=moved, transcendentals=0),
            compiler_params=pltpu.CompilerParams(vmem_limit_bytes=LIMIT),
        )(*args)

    return call


def swapped(block):
    return lax.ppermute(
        block, "col", [(c, (c + (2 if c % 2 else -2)) % N_COL) for c in range(N_COL)]
    )


def swapped_back(block):
    return lax.ppermute(
        block, "col", [(c, (c + (-2 if c % 2 else 2)) % N_COL) for c in range(N_COL)]
    )


def exchange(pieces, axis):
    n = lax.axis_size(axis)
    rows = pieces.shape[0] // n
    shape = (n, rows, 128) if rows in (4, 8) else (n, 1, rows * 128)
    return lax.all_to_all(pieces.reshape(shape), axis, 0, 0, tiled=True).reshape(pieces.shape)


def on_device(matrix, seats):
    total_rows = matrix.shape[0] * N_ROW
    one = 6 * W**3
    fold_all = local(functools.partial(fold, total_rows), 1, (8 * N_ROW, 128))
    sent = local(pack_first, one, (PIECE * N_ROW, 128))(matrix)
    tiles = exchange(fold_all(exchange(sent, "row")), "row")
    move = local(first_move, 5 * one, (W, W))(matrix, tiles)
    guest = swapped(move)
    keep = local(first_keep, 5 * one, (W, W))(matrix, tiles)
    sent = local(pack_second, one, (PIECE * N_ROW, 128))(keep, guest)
    tiles = exchange(fold_all(exchange(sent, "row")), "row")
    keep, guest, sums = local(second, 10 * one, (W, W), (W, W), (4 * N_ROW, 128))(keep, guest, tiles)
    back = swapped_back(guest)
    sums = exchange(sums, "row")
    means = local(functools.partial(fold_sums, total_rows), 1, (4 * N_COL, 128))(sums)
    table = exchange(means, "col").reshape(N_COL, 4, 128)
    odd = lax.axis_index("col") % 2 == 1
    final = jnp.concatenate([jnp.where(odd, back, keep), jnp.where(odd, keep, back)], axis=1)
    kept = table[:, :2].reshape(N_COL, W)
    guests = table[:, 2:].reshape(N_COL, W)
    rows = []
    for c in range(N_COL):
        rows.append(guests[(c + 2) % N_COL] if c % 2 else kept[c])
        rows.append(kept[c] if c % 2 else guests[(c - 2) % N_COL])
    by_seat = jnp.stack(rows)
    wanted = 2 * lax.axis_index("col") + jnp.arange(2, dtype=jnp.int32)
    hit = seats[None, :] == wanted[:, None]
    picked = jnp.sum(jnp.where(hit[:, :, None], by_seat[None], 0.0), axis=1)
    return (final, picked.reshape(2 * W))


def solution(mesh):
    placed = (P("row", "col"), P())
    return jax.shard_map(
        on_device,
        mesh=mesh,
        in_specs=placed,
        out_specs=(P("row", "col"), P("col")),
        check_vma=False,
    )
```

```python
import functools

import jax
import jax.numpy as jnp
from jax import lax
from jax.experimental import pallas as pl
from jax.experimental.pallas import tpu as pltpu
from jax.sharding import PartitionSpec as P

W = 256
N_ROW = 64
N_COL = 8
PIECE = 10
WIDE = 17
LIMIT = 32 * 1024 * 1024


def split(a):
    high = a.astype(jnp.bfloat16)
    return high, (a - high.astype(jnp.float32)).astype(jnp.bfloat16)


def product(a, b, ca=1, cb=0):
    def one(p, q):
        return lax.dot_general(
            p, q, (((ca,), (cb,)), ((), ())), preferred_element_type=jnp.float32
        )

    return one(a[0], b[0]) + (one(a[0], b[1]) + one(a[1], b[0]))


def root(s, also):
    parts = split(s)
    s2 = product(parts, parts)
    other = also()
    rows = lax.broadcasted_iota(jnp.int32, s.shape, 0)
    cols = lax.broadcasted_iota(jnp.int32, s.shape, 1)
    eye = jnp.where(rows == cols, 1.0, 0.0).astype(jnp.float32)
    base = eye - 0.5 * s + 0.375 * s2
    return base + product(split(s2), split(0.0625 * s2 - 0.3125 * s)), other


def tile_at(block, r):
    i, half = r % 32, r // 32
    return block[8 * i : 8 * i + 8, 128 * half : 128 * half + 128]


def from_tiles(ref, first, step):
    left = [ref[step * r + first : step * r + first + 8, :] for r in range(32)]
    right = [ref[step * r + first : step * r + first + 8, :] for r in range(32, 64)]
    return jnp.concatenate(
        [jnp.concatenate(left, axis=0), jnp.concatenate(right, axis=0)], axis=1
    )


def column_squares(block):
    return jnp.sum(block * block, axis=0, keepdims=True)


def halves(matrix):
    odd = lax.rem(lax.axis_index("col"), 2)
    keep = matrix[:, pl.ds(pl.multiple_of(odd * W, W), W)]
    move = matrix[:, pl.ds(pl.multiple_of((1 - odd) * W, W), W)]
    return keep, move


def pack_first(matrix, out):
    keep, move = halves(matrix)
    cross = product(split(keep), split(move), 0, 0)
    norm_keep, norm_move = column_squares(keep), column_squares(move)
    for r in range(N_ROW):
        i, half = r % 32, r // 32
        at = PIECE * r
        out[at : at + 8, :] = tile_at(cross, r)
        out[at + 8 : at + 9, :] = norm_keep[:, 128 * (i // 16) : 128 * (i // 16) + 128]
        out[at + 9 : at + 10, :] = norm_move[:, 128 * half : 128 * half + 128]


def square_index():
    rows = lax.broadcasted_iota(jnp.int32, (W, W), 0)
    return rows, lax.broadcasted_iota(jnp.int32, (W, W), 1)


def pack_second(keep, guest, gram_keep, out):
    parts = split(guest[...])
    cross = product(split(keep[...]), parts, 0, 0)
    rows, cols = square_index()
    grams = jnp.where(rows <= cols, gram_keep[...], product(parts, parts, 0, 0))
    norm_guest = column_squares(guest[...])
    for r in range(N_ROW):
        half, at = r // 32, WIDE * r
        out[at : at + 8, :] = tile_at(cross, r)
        out[at + 8 : at + 16, :] = tile_at(grams, r)
        out[at + 16 : at + 17, :] = norm_guest[:, 128 * half : 128 * half + 128]


def fold(total_rows, got, out):
    tile = got[0:8, :]
    norms = got[8:10, :]
    for r in range(1, N_ROW):
        tile += got[PIECE * r : PIECE * r + 8, :]
        norms += got[PIECE * r + 8 : PIECE * r + 10, :]
    sign = jnp.where(lax.rem(lax.axis_index("col"), 2) == 1, -0.5, 0.5)
    first = 8 * lax.rem(lax.axis_index("row"), 16)
    lanes = lax.broadcasted_iota(jnp.int32, (8, 128), 1)
    rows = lax.broadcasted_iota(jnp.int32, (8, 128), 0)
    means = norms / total_rows
    mean_keep = jnp.sum(
        jnp.where(lanes == first + rows, means[0:1], 0.0), axis=1, keepdims=True
    )
    x = sign * (tile / total_rows) / jnp.sqrt((mean_keep + 1e-06) * (means[1:2] + 1e-06))
    for r in range(N_ROW):
        out[8 * r : 8 * r + 8, :] = x


def fold_wide(got, out):
    piece = got[0:WIDE, :]
    for r in range(1, N_ROW):
        piece += got[WIDE * r : WIDE * r + WIDE, :]
    for r in range(N_ROW):
        out[WIDE * r : WIDE * r + WIDE, :] = piece


def first_move(matrix, tiles, out):
    keep, move = halves(matrix)
    x = split(from_tiles(tiles, 0, 8))
    z, mixed = root(product(x, x, 0, 0), lambda: move + product(split(keep), x))
    out[...] = product(split(mixed), split(z))


def first_keep(matrix, tiles, out, gram):
    keep, move = halves(matrix)
    x = split(from_tiles(tiles, 0, 8))
    z, mixed = root(product(x, x, 1, 1), lambda: keep - product(split(move), x, 1, 1))
    kept = product(split(mixed), split(z))
    out[...] = kept
    parts = split(kept)
    gram[...] = product(parts, parts, 0, 0)


def guest_squares(got):
    at = 32 * WIDE + 16
    return jnp.concatenate([got[16:17, :], got[at : at + 1, :]], axis=1)


def second_guest(total_rows, keep, guest, got, new_guest, x_out, z_out):
    cross = from_tiles(got, 0, WIDE)
    rows, cols = square_index()
    on_diagonal = jnp.where(rows == cols, from_tiles(got, 8, WIDE), 0.0)
    mean_keep = jnp.sum(on_diagonal, axis=1, keepdims=True) / total_rows
    mean_guest = guest_squares(got) / total_rows
    sign = jnp.where(lax.rem(lax.axis_index("col"), 2) == 1, -0.5, 0.5) / total_rows
    x = cross * (sign * lax.rsqrt(mean_keep + 1e-06)) * lax.rsqrt(mean_guest + 1e-06)
    x_out[...] = x
    x = split(x)
    z, mixed = root(product(x, x, 0, 0), lambda: guest[...] + product(split(keep[...]), x))
    z_out[...] = z
    new_guest[...] = product(split(mixed), split(z))


def second_sums(total_rows, x_in, z_guest_in, got, z_out, sums):
    x = split(x_in[...])
    z, _ = root(product(x, x, 1, 1), lambda: None)
    z_out[...] = z
    cross = split(from_tiles(got, 0, WIDE))
    grams = from_tiles(got, 8, WIDE)
    flipped = grams.T
    rows, cols = square_index()
    of_keep = split(jnp.where(rows <= cols, grams, flipped))
    of_guest = jnp.where(rows > cols, grams, flipped)
    of_guest = split(jnp.where(rows == cols, guest_squares(got), of_guest))
    z_guest = z_guest_in[...]
    zs, zs_guest = split(z), split(z_guest)
    v = product(x, zs, 0, 0)
    w = product(x, zs_guest)
    vs, ws = split(v), split(w)
    sum_keep = jnp.sum(
        z * (product(of_keep, zs) - 2.0 * product(cross, vs)) + v * product(of_guest, vs),
        axis=0,
        keepdims=True,
    )
    sum_guest = jnp.sum(
        z_guest * product(of_guest, zs_guest)
        + w * (product(of_keep, ws) + 2.0 * product(cross, zs_guest)),
        axis=0,
        keepdims=True,
    )
    four = [sum_keep[:, :128], sum_keep[:, 128:], sum_guest[:, :128], sum_guest[:, 128:]]
    tile = jnp.maximum(jnp.concatenate(four + four, axis=0) / total_rows, 0.0)
    for r in range(4 * N_COL // 8):
        sums[8 * r : 8 * r + 8, :] = tile


def second_keep(keep, guest, x_in, z_in, out):
    x = split(x_in[...])
    mixed = keep[...] - product(split(guest[...]), x, 1, 1)
    out[...] = product(split(mixed), split(z_in[...]))


def local(body, flops, *shapes):
    out = [jax.ShapeDtypeStruct(shape, jnp.float32) for shape in shapes]

    def call(*args):
        moved = sum(4 * a.size for a in args) + sum(4 * s.size for s in out)
        return pl.pallas_call(
            body,
            out_shape=out if len(out) > 1 else out[0],
            in_specs=[pl.BlockSpec(memory_space=pltpu.VMEM)] * len(args),
            out_specs=[pl.BlockSpec(memory_space=pltpu.VMEM)] * len(out)
            if len(out) > 1
            else pl.BlockSpec(memory_space=pltpu.VMEM),
            cost_estimate=pl.CostEstimate(flops=flops, bytes_accessed=moved, transcendentals=0),
            compiler_params=pltpu.CompilerParams(vmem_limit_bytes=LIMIT),
        )(*args)

    return call


def swapped(block):
    return lax.ppermute(
        block, "col", [(c, (c + (2 if c % 2 else -2)) % N_COL) for c in range(N_COL)]
    )


def swapped_back(block):
    return lax.ppermute(
        block, "col", [(c, (c + (-2 if c % 2 else 2)) % N_COL) for c in range(N_COL)]
    )


def exchange(pieces, axis):
    n = lax.axis_size(axis)
    rows = pieces.shape[0] // n
    shape = (n, rows, 128) if rows in (4, 8) else (n, 1, rows * 128)
    return lax.all_to_all(pieces.reshape(shape), axis, 0, 0, tiled=True).reshape(pieces.shape)


def on_device(matrix, seats):
    total_rows = matrix.shape[0] * N_ROW
    one = 6 * W**3
    fold_all = local(functools.partial(fold, total_rows), 1, (8 * N_ROW, 128))
    sent = local(pack_first, one, (PIECE * N_ROW, 128))(matrix)
    tiles = exchange(fold_all(exchange(sent, "row")), "row")
    move = local(first_move, 5 * one, (W, W))(matrix, tiles)
    guest = swapped(move)
    keep, gram = local(first_keep, 6 * one, (W, W), (W, W))(matrix, tiles)
    sent = local(pack_second, 2 * one, (WIDE * N_ROW, 128))(keep, guest, gram)
    folded = local(fold_wide, 1, (WIDE * N_ROW, 128))(exchange(sent, "row"))
    got = exchange(folded, "row")
    new_guest, x, z_guest = local(
        functools.partial(second_guest, total_rows), 5 * one, (W, W), (W, W), (W, W)
    )(keep, guest, got)
    back = swapped_back(new_guest)
    z, means = local(
        functools.partial(second_sums, total_rows), 11 * one, (W, W), (4 * N_COL, 128)
    )(x, z_guest, got)
    table = exchange(means, "col").reshape(N_COL, 4, 128)
    keep = local(second_keep, 2 * one, (W, W))(keep, guest, x, z)
    odd = lax.axis_index("col") % 2 == 1
    final = jnp.concatenate([jnp.where(odd, back, keep), jnp.where(odd, keep, back)], axis=1)
    kept = table[:, :2].reshape(N_COL, W)
    guests = table[:, 2:].reshape(N_COL, W)
    rows = []
    for c in range(N_COL):
        rows.append(guests[(c + 2) % N_COL] if c % 2 else kept[c])
        rows.append(kept[c] if c % 2 else guests[(c - 2) % N_COL])
    by_seat = jnp.stack(rows)
    wanted = 2 * lax.axis_index("col") + jnp.arange(2, dtype=jnp.int32)
    hit = seats[None, :] == wanted[:, None]
    picked = jnp.sum(jnp.where(hit[:, :, None], by_seat[None], 0.0), axis=1)
    return (final, picked.reshape(2 * W))


def solution(mesh):
    placed = (P("row", "col"), P())
    return jax.shard_map(
        on_device,
        mesh=mesh,
        in_specs=placed,
        out_specs=(P("row", "col"), P("col")),
        check_vma=False,
    )
```

```python
import functools

import jax
import jax.numpy as jnp
from jax import lax
from jax.experimental import pallas as pl
from jax.experimental.pallas import tpu as pltpu
from jax.sharding import PartitionSpec as P

W = 256
N_ROW = 64
N_COL = 8
PIECE = 10
WIDE = 17
LOADS = 8
LIMIT = 32 * 1024 * 1024
LOAD_LIMIT = 56000000


def split(a):
    high = a.astype(jnp.bfloat16)
    return high, (a - high.astype(jnp.float32)).astype(jnp.bfloat16)


def product(a, b, ca=1, cb=0):
    def one(p, q):
        return lax.dot_general(
            p, q, (((ca,), (cb,)), ((), ())), preferred_element_type=jnp.float32
        )

    return one(a[0], b[0]) + (one(a[0], b[1]) + one(a[1], b[0]))


def root(s, also):
    parts = split(s)
    s2 = product(parts, parts)
    other = also()
    rows = lax.broadcasted_iota(jnp.int32, s.shape, 0)
    cols = lax.broadcasted_iota(jnp.int32, s.shape, 1)
    eye = jnp.where(rows == cols, 1.0, 0.0).astype(jnp.float32)
    base = eye - 0.5 * s + 0.375 * s2
    return base + product(split(s2), split(0.0625 * s2 - 0.3125 * s)), other


def tile_at(block, r):
    i, half = r % 32, r // 32
    return block[8 * i : 8 * i + 8, 128 * half : 128 * half + 128]


def from_tiles(ref, first, step):
    left = [ref[step * r + first : step * r + first + 8, :] for r in range(32)]
    right = [ref[step * r + first : step * r + first + 8, :] for r in range(32, 64)]
    return jnp.concatenate(
        [jnp.concatenate(left, axis=0), jnp.concatenate(right, axis=0)], axis=1
    )


def column_squares(block):
    return jnp.sum(block * block, axis=0, keepdims=True)


def halves(matrix):
    odd = lax.rem(lax.axis_index("col"), 2)
    keep = matrix[:, pl.ds(pl.multiple_of(odd * W, W), W)]
    move = matrix[:, pl.ds(pl.multiple_of((1 - odd) * W, W), W)]
    return keep, move


def pack_first(whole, out, matrix, arrived):
    rows = W // LOADS
    copies = [
        pltpu.make_async_copy(
            whole.at[pl.ds(k * rows, rows)], matrix.at[pl.ds(k * rows, rows)], arrived.at[k]
        )
        for k in range(LOADS)
    ]
    for copy in copies:
        copy.start()
    for copy in copies:
        copy.wait()
    keep, move = halves(matrix)
    cross = product(split(keep), split(move), 0, 0)
    norm_keep, norm_move = column_squares(keep), column_squares(move)
    for r in range(N_ROW):
        i, half = r % 32, r // 32
        at = PIECE * r
        out[at : at + 8, :] = tile_at(cross, r)
        out[at + 8 : at + 9, :] = norm_keep[:, 128 * (i // 16) : 128 * (i // 16) + 128]
        out[at + 9 : at + 10, :] = norm_move[:, 128 * half : 128 * half + 128]


def square_index():
    rows = lax.broadcasted_iota(jnp.int32, (W, W), 0)
    return rows, lax.broadcasted_iota(jnp.int32, (W, W), 1)


def pack_second(keep, guest, gram_keep, out):
    parts = split(guest[...])
    cross = product(split(keep[...]), parts, 0, 0)
    rows, cols = square_index()
    grams = jnp.where(rows <= cols, gram_keep[...], product(parts, parts, 0, 0))
    norm_guest = column_squares(guest[...])
    for r in range(N_ROW):
        half, at = r // 32, WIDE * r
        out[at : at + 8, :] = tile_at(cross, r)
        out[at + 8 : at + 16, :] = tile_at(grams, r)
        out[at + 16 : at + 17, :] = norm_guest[:, 128 * half : 128 * half + 128]


def fold(total_rows, got, out):
    tile = got[0:8, :]
    norms = got[8:10, :]
    for r in range(1, N_ROW):
        tile += got[PIECE * r : PIECE * r + 8, :]
        norms += got[PIECE * r + 8 : PIECE * r + 10, :]
    sign = jnp.where(lax.rem(lax.axis_index("col"), 2) == 1, -0.5, 0.5)
    first = 8 * lax.rem(lax.axis_index("row"), 16)
    lanes = lax.broadcasted_iota(jnp.int32, (8, 128), 1)
    rows = lax.broadcasted_iota(jnp.int32, (8, 128), 0)
    means = norms / total_rows
    mean_keep = jnp.sum(
        jnp.where(lanes == first + rows, means[0:1], 0.0), axis=1, keepdims=True
    )
    x = sign * (tile / total_rows) / jnp.sqrt((mean_keep + 1e-06) * (means[1:2] + 1e-06))
    for r in range(N_ROW):
        out[8 * r : 8 * r + 8, :] = x


def fold_wide(got, out):
    piece = got[0:WIDE, :]
    for r in range(1, N_ROW):
        piece += got[WIDE * r : WIDE * r + WIDE, :]
    for r in range(N_ROW):
        out[WIDE * r : WIDE * r + WIDE, :] = piece


def first_move(matrix, tiles, out):
    keep, move = halves(matrix)
    x = split(from_tiles(tiles, 0, 8))
    z, mixed = root(product(x, x, 0, 0), lambda: move + product(split(keep), x))
    out[...] = product(split(mixed), split(z))


def first_keep(matrix, tiles, seats, out, gram, hits):
    first = 2 * lax.axis_index("col")
    for k in range(2):
        for seat in range(2 * N_COL):
            at = 2 * N_COL * k + seat
            hit = jnp.where(seats[seat] == first + k, 1.0, 0.0).astype(jnp.float32)
            hits[at : at + 1, :] = jnp.full((1, 128), hit)
    keep, move = halves(matrix)
    x = split(from_tiles(tiles, 0, 8))
    z, mixed = root(product(x, x, 1, 1), lambda: keep - product(split(move), x, 1, 1))
    kept = product(split(mixed), split(z))
    out[...] = kept
    parts = split(kept)
    gram[...] = product(parts, parts, 0, 0)


def guest_squares(got):
    at = 32 * WIDE + 16
    return jnp.concatenate([got[16:17, :], got[at : at + 1, :]], axis=1)


def second_guest(total_rows, keep, guest, got, new_guest, x_out, z_out):
    cross = from_tiles(got, 0, WIDE)
    rows, cols = square_index()
    on_diagonal = jnp.where(rows == cols, from_tiles(got, 8, WIDE), 0.0)
    mean_keep = jnp.sum(on_diagonal, axis=1, keepdims=True) / total_rows
    mean_guest = guest_squares(got) / total_rows
    sign = jnp.where(lax.rem(lax.axis_index("col"), 2) == 1, -0.5, 0.5) / total_rows
    x = cross * (sign * lax.rsqrt(mean_keep + 1e-06)) * lax.rsqrt(mean_guest + 1e-06)
    x_out[...] = x
    x = split(x)
    z, mixed = root(product(x, x, 0, 0), lambda: guest[...] + product(split(keep[...]), x))
    z_out[...] = z
    new_guest[...] = product(split(mixed), split(z))


def half_of(ref, odd):
    return ref.at[:, pl.ds(pl.multiple_of(odd * W, W), W)]


def second_sums(total_rows, x_in, z_guest_in, got, keep, guest, sums, final, kept, done):
    x = split(x_in[...])
    z, mixed = root(
        product(x, x, 1, 1), lambda: keep[...] - product(split(guest[...]), x, 1, 1)
    )
    zs = split(z)
    kept[...] = product(split(mixed), zs)
    odd = lax.rem(lax.axis_index("col"), 2)
    copy = pltpu.make_async_copy(kept, half_of(final, odd), done)
    copy.start()
    cross = split(from_tiles(got, 0, WIDE))
    grams = from_tiles(got, 8, WIDE)
    flipped = grams.T
    rows, cols = square_index()
    of_keep = split(jnp.where(rows <= cols, grams, flipped))
    of_guest = jnp.where(rows > cols, grams, flipped)
    of_guest = split(jnp.where(rows == cols, guest_squares(got), of_guest))
    z_guest = z_guest_in[...]
    zs_guest = split(z_guest)
    v = product(x, zs, 0, 0)
    w = product(x, zs_guest)
    vs, ws = split(v), split(w)
    sum_keep = jnp.sum(
        z * (product(of_keep, zs) - 2.0 * product(cross, vs)) + v * product(of_guest, vs),
        axis=0,
        keepdims=True,
    )
    sum_guest = jnp.sum(
        z_guest * product(of_guest, zs_guest)
        + w * (product(of_keep, ws) + 2.0 * product(cross, zs_guest)),
        axis=0,
        keepdims=True,
    )
    four = [sum_keep[:, :128], sum_keep[:, 128:], sum_guest[:, :128], sum_guest[:, 128:]]
    tile = jnp.maximum(jnp.concatenate(four + four, axis=0) / total_rows, 0.0)
    for r in range(4 * N_COL // 8):
        sums[8 * r : 8 * r + 8, :] = tile
    copy.wait()


def finish(hits, back, table, begun, final, means, done):
    del begun
    col = lax.axis_index("col")
    copy = pltpu.make_async_copy(back, half_of(final, 1 - lax.rem(col, 2)), done)
    copy.start()
    for k in range(2):
        picked = jnp.zeros((2, 128), jnp.float32)
        for c in range(N_COL):
            kept = table[4 * c : 4 * c + 2, :]
            at = 4 * ((c + (2 if c % 2 else -2)) % N_COL) + 2
            hosted = table[at : at + 2, :]
            for b, part in enumerate((hosted, kept) if c % 2 else (kept, hosted)):
                seat = 2 * N_COL * k + 2 * c + b
                picked += jnp.where(hits[seat : seat + 1, :] > 0.5, part, 0.0)
        means[2 * k : 2 * k + 2, :] = picked
    copy.wait()


VMEM = pl.BlockSpec(memory_space=pltpu.VMEM)
SMEM = pl.BlockSpec(memory_space=pltpu.SMEM)
HBM = pl.BlockSpec(memory_space=pltpu.HBM)


def local(body, flops, *shapes, ins=None, outs=None, scratch=(), aliases=None, limit=LIMIT):
    out = [jax.ShapeDtypeStruct(shape, jnp.float32) for shape in shapes]
    outs = outs or [VMEM] * len(out)
    one = len(out) == 1

    def call(*args):
        moved = sum(4 * a.size for a in args) + sum(4 * s.size for s in out)
        return pl.pallas_call(
            body,
            out_shape=out[0] if one else out,
            in_specs=ins or [VMEM] * len(args),
            out_specs=outs[0] if one else outs,
            scratch_shapes=scratch,
            input_output_aliases=aliases or {},
            cost_estimate=pl.CostEstimate(flops=flops, bytes_accessed=moved, transcendentals=0),
            compiler_params=pltpu.CompilerParams(vmem_limit_bytes=limit),
        )(*args)

    return call


def swapped(block):
    return lax.ppermute(
        block, "col", [(c, (c + (2 if c % 2 else -2)) % N_COL) for c in range(N_COL)]
    )


def swapped_back(block):
    return lax.ppermute(
        block, "col", [(c, (c + (-2 if c % 2 else 2)) % N_COL) for c in range(N_COL)]
    )


def exchange(pieces, axis):
    n = lax.axis_size(axis)
    rows = pieces.shape[0] // n
    shape = (n, rows, 128) if rows in (4, 8) else (n, 1, rows * 128)
    return lax.all_to_all(pieces.reshape(shape), axis, 0, 0, tiled=True).reshape(pieces.shape)


def on_device(matrix, seats):
    total_rows = matrix.shape[0] * N_ROW
    one = 6 * W**3
    fold_all = local(functools.partial(fold, total_rows), 1, (8 * N_ROW, 128))
    sent = local(
        pack_first,
        one,
        (PIECE * N_ROW, 128),
        ins=[HBM],
        limit=LOAD_LIMIT,
        scratch=[pltpu.VMEM((W, 2 * W), jnp.float32), pltpu.SemaphoreType.DMA((LOADS,))],
    )(matrix)
    tiles = exchange(fold_all(exchange(sent, "row")), "row")
    move = local(first_move, 5 * one, (W, W))(matrix, tiles)
    guest = swapped(move)
    keep, gram, hits = local(
        first_keep, 6 * one, (W, W), (W, W), (4 * N_COL, 128), ins=[VMEM, VMEM, SMEM]
    )(matrix, tiles, seats)
    sent = local(pack_second, 2 * one, (WIDE * N_ROW, 128))(keep, guest, gram)
    folded = local(fold_wide, 1, (WIDE * N_ROW, 128))(exchange(sent, "row"))
    got = exchange(folded, "row")
    new_guest, x, z_guest = local(
        functools.partial(second_guest, total_rows), 5 * one, (W, W), (W, W), (W, W)
    )(keep, guest, got)
    back = swapped_back(new_guest)
    means, begun = local(
        functools.partial(second_sums, total_rows),
        13 * one,
        (4 * N_COL, 128),
        (W, 2 * W),
        outs=[VMEM, HBM],
        scratch=[pltpu.VMEM((W, W), jnp.float32), pltpu.SemaphoreType.DMA],
    )(x, z_guest, got, keep, guest)
    table = exchange(means, "col")
    final, picked = local(
        finish,
        1,
        (W, 2 * W),
        (4, 128),
        ins=[VMEM, VMEM, VMEM, HBM],
        outs=[HBM, VMEM],
        scratch=[pltpu.SemaphoreType.DMA],
        aliases={3: 0},
    )(hits, back, table, begun)
    return (final, picked.reshape(2 * W))


def solution(mesh):
    placed = (P("row", "col"), P())
    return jax.shard_map(
        on_device,
        mesh=mesh,
        in_specs=placed,
        out_specs=(P("row", "col"), P("col")),
        check_vma=False,
    )
```

```python
import functools

import jax
import jax.numpy as jnp
from jax import lax
from jax.experimental import pallas as pl
from jax.experimental.pallas import tpu as pltpu
from jax.sharding import PartitionSpec as P

W = 256
N_ROW = 64
N_COL = 8
PIECE = 10
WIDE = 17
LOADS = 8
LIMIT = 32 * 1024 * 1024
LOAD_LIMIT = 56000000


def split(a):
    high = a.astype(jnp.bfloat16)
    return high, (a - high.astype(jnp.float32)).astype(jnp.bfloat16)


def product(a, b, ca=1, cb=0):
    def one(p, q):
        return lax.dot_general(
            p, q, (((ca,), (cb,)), ((), ())), preferred_element_type=jnp.float32
        )

    return one(a[0], b[0]) + (one(a[0], b[1]) + one(a[1], b[0]))


def root(s, also):
    parts = split(s)
    s2 = product(parts, parts)
    other = also()
    rows = lax.broadcasted_iota(jnp.int32, s.shape, 0)
    cols = lax.broadcasted_iota(jnp.int32, s.shape, 1)
    eye = jnp.where(rows == cols, 1.0, 0.0).astype(jnp.float32)
    base = eye - 0.5 * s + 0.375 * s2
    return base + product(split(s2), split(0.0625 * s2 - 0.3125 * s)), other


def tile_at(block, r):
    i, half = r % 32, r // 32
    return block[8 * i : 8 * i + 8, 128 * half : 128 * half + 128]


def from_tiles(ref, first, step):
    left = [ref[step * r + first : step * r + first + 8, :] for r in range(32)]
    right = [ref[step * r + first : step * r + first + 8, :] for r in range(32, 64)]
    return jnp.concatenate(
        [jnp.concatenate(left, axis=0), jnp.concatenate(right, axis=0)], axis=1
    )


def roots(*squares):
    parts = [split(s) for s in squares]
    seconds = [product(p, p) for p in parts]
    rows, cols = square_index()
    eye = jnp.where(rows == cols, 1.0, 0.0).astype(jnp.float32)
    return [
        eye - 0.5 * s + 0.375 * s2 + product(split(s2), split(0.0625 * s2 - 0.3125 * s))
        for s, s2 in zip(squares, seconds)
    ]


def column_squares(block):
    return jnp.sum(block * block, axis=0, keepdims=True)


def halves(matrix):
    odd = lax.rem(lax.axis_index("col"), 2)
    keep = matrix[:, pl.ds(pl.multiple_of(odd * W, W), W)]
    move = matrix[:, pl.ds(pl.multiple_of((1 - odd) * W, W), W)]
    return keep, move


def pack_first(whole, out, matrix, arrived):
    rows = W // LOADS
    copies = [
        pltpu.make_async_copy(
            whole.at[pl.ds(k * rows, rows)], matrix.at[pl.ds(k * rows, rows)], arrived.at[k]
        )
        for k in range(LOADS)
    ]
    for copy in copies:
        copy.start()
    for copy in copies:
        copy.wait()
    keep, move = halves(matrix)
    cross = product(split(keep), split(move), 0, 0)
    norm_keep, norm_move = column_squares(keep), column_squares(move)
    for r in range(N_ROW):
        i, half = r % 32, r // 32
        at = PIECE * r
        out[at : at + 8, :] = tile_at(cross, r)
        out[at + 8 : at + 9, :] = norm_keep[:, 128 * (i // 16) : 128 * (i // 16) + 128]
        out[at + 9 : at + 10, :] = norm_move[:, 128 * half : 128 * half + 128]


def square_index():
    rows = lax.broadcasted_iota(jnp.int32, (W, W), 0)
    return rows, lax.broadcasted_iota(jnp.int32, (W, W), 1)


def pack_second(keep, guest, gram_keep, out):
    parts = split(guest[...])
    cross = product(split(keep[...]), parts, 0, 0)
    rows, cols = square_index()
    grams = jnp.where(rows <= cols, gram_keep[...], product(parts, parts, 0, 0))
    norm_guest = column_squares(guest[...])
    for r in range(N_ROW):
        half, at = r // 32, WIDE * r
        out[at : at + 8, :] = tile_at(cross, r)
        out[at + 8 : at + 16, :] = tile_at(grams, r)
        out[at + 16 : at + 17, :] = norm_guest[:, 128 * half : 128 * half + 128]


def fold(total_rows, got, out):
    tile = got[0:8, :]
    norms = got[8:10, :]
    for r in range(1, N_ROW):
        tile += got[PIECE * r : PIECE * r + 8, :]
        norms += got[PIECE * r + 8 : PIECE * r + 10, :]
    sign = jnp.where(lax.rem(lax.axis_index("col"), 2) == 1, -0.5, 0.5)
    first = 8 * lax.rem(lax.axis_index("row"), 16)
    lanes = lax.broadcasted_iota(jnp.int32, (8, 128), 1)
    rows = lax.broadcasted_iota(jnp.int32, (8, 128), 0)
    means = norms / total_rows
    mean_keep = jnp.sum(
        jnp.where(lanes == first + rows, means[0:1], 0.0), axis=1, keepdims=True
    )
    x = sign * (tile / total_rows) / jnp.sqrt((mean_keep + 1e-06) * (means[1:2] + 1e-06))
    for r in range(N_ROW):
        out[8 * r : 8 * r + 8, :] = x


def fold_wide(got, out):
    piece = got[0:WIDE, :]
    for r in range(1, N_ROW):
        piece += got[WIDE * r : WIDE * r + WIDE, :]
    for r in range(N_ROW):
        out[WIDE * r : WIDE * r + WIDE, :] = piece


def first_move(matrix, tiles, out):
    keep, move = halves(matrix)
    x = split(from_tiles(tiles, 0, 8))
    z, mixed = root(product(x, x, 0, 0), lambda: move + product(split(keep), x))
    out[...] = product(split(mixed), split(z))


def first_keep(matrix, tiles, seats, out, gram, hits):
    first = 2 * lax.axis_index("col")
    for k in range(2):
        for seat in range(2 * N_COL):
            at = 2 * N_COL * k + seat
            hit = jnp.where(seats[seat] == first + k, 1.0, 0.0).astype(jnp.float32)
            hits[at : at + 1, :] = jnp.full((1, 128), hit)
    keep, move = halves(matrix)
    x = split(from_tiles(tiles, 0, 8))
    z, mixed = root(product(x, x, 1, 1), lambda: keep - product(split(move), x, 1, 1))
    kept = product(split(mixed), split(z))
    out[...] = kept
    parts = split(kept)
    gram[...] = product(parts, parts, 0, 0)


def guest_squares(got):
    at = 32 * WIDE + 16
    return jnp.concatenate([got[16:17, :], got[at : at + 1, :]], axis=1)


def second_guest(total_rows, keep, guest, got, new_guest, x_out, z_keep_out, z_guest_out):
    cross = from_tiles(got, 0, WIDE)
    rows, cols = square_index()
    on_diagonal = jnp.where(rows == cols, from_tiles(got, 8, WIDE), 0.0)
    mean_keep = jnp.sum(on_diagonal, axis=1, keepdims=True) / total_rows
    mean_guest = guest_squares(got) / total_rows
    sign = jnp.where(lax.rem(lax.axis_index("col"), 2) == 1, -0.5, 0.5) / total_rows
    x = cross * (sign * lax.rsqrt(mean_keep + 1e-06)) * lax.rsqrt(mean_guest + 1e-06)
    x_out[...] = x
    flipped = split(x.T)
    x = split(x)
    s_guest = product(flipped, flipped, 1, 1)
    s_keep = product(x, x, 1, 1)
    mixed = guest[...] + product(split(keep[...]), x)
    z_guest, z_keep = roots(s_guest, s_keep)
    z_guest_out[...] = z_guest
    z_keep_out[...] = z_keep
    new_guest[...] = product(split(mixed), split(z_guest))


def half_of(ref, odd):
    return ref.at[:, pl.ds(pl.multiple_of(odd * W, W), W)]


def second_sums(
    total_rows, x_in, z_keep_in, z_guest_in, got, keep, guest, sums, final, kept, done
):
    x = x_in[...]
    flipped_x = split(x.T)
    x = split(x)
    z = z_keep_in[...]
    zs = split(z)
    mixed = keep[...] - product(split(guest[...]), x, 1, 1)
    kept[...] = product(split(mixed), zs)
    odd = lax.rem(lax.axis_index("col"), 2)
    copy = pltpu.make_async_copy(kept, half_of(final, odd), done)
    copy.start()
    cross = split(from_tiles(got, 0, WIDE))
    grams = from_tiles(got, 8, WIDE)
    flipped = grams.T
    rows, cols = square_index()
    of_keep = split(jnp.where(rows <= cols, grams, flipped))
    of_guest = jnp.where(rows > cols, grams, flipped)
    of_guest = split(jnp.where(rows == cols, guest_squares(got), of_guest))
    z_guest = z_guest_in[...]
    zs_guest = split(z_guest)
    v = product(flipped_x, zs)
    w = product(x, zs_guest)
    vs, ws = split(v), split(w)
    sum_keep = jnp.sum(
        z * (product(of_keep, zs) - 2.0 * product(cross, vs)) + v * product(of_guest, vs),
        axis=0,
        keepdims=True,
    )
    sum_guest = jnp.sum(
        z_guest * product(of_guest, zs_guest)
        + w * (product(of_keep, ws) + 2.0 * product(cross, zs_guest)),
        axis=0,
        keepdims=True,
    )
    four = [sum_keep[:, :128], sum_keep[:, 128:], sum_guest[:, :128], sum_guest[:, 128:]]
    tile = jnp.maximum(jnp.concatenate(four + four, axis=0) / total_rows, 0.0)
    for r in range(4 * N_COL // 8):
        sums[8 * r : 8 * r + 8, :] = tile
    copy.wait()


def finish(hits, back, table, begun, final, means, picked, done):
    del begun
    col = lax.axis_index("col")
    copy = pltpu.make_async_copy(back, half_of(final, 1 - lax.rem(col, 2)), done.at[0])
    copy.start()
    for k in range(2):
        one = jnp.zeros((2, 128), jnp.float32)
        for c in range(N_COL):
            kept = table[4 * c : 4 * c + 2, :]
            at = 4 * ((c + (2 if c % 2 else -2)) % N_COL) + 2
            hosted = table[at : at + 2, :]
            for b, part in enumerate((hosted, kept) if c % 2 else (kept, hosted)):
                seat = 2 * N_COL * k + 2 * c + b
                one += jnp.where(hits[seat : seat + 1, :] > 0.5, part, 0.0)
        picked[2 * k : 2 * k + 2, :] = one
    means_copy = pltpu.make_async_copy(picked, means, done.at[1])
    means_copy.start()
    copy.wait()
    means_copy.wait()


VMEM = pl.BlockSpec(memory_space=pltpu.VMEM)
SMEM = pl.BlockSpec(memory_space=pltpu.SMEM)
HBM = pl.BlockSpec(memory_space=pltpu.HBM)


def local(body, flops, *shapes, ins=None, outs=None, scratch=(), aliases=None, limit=LIMIT):
    out = [jax.ShapeDtypeStruct(shape, jnp.float32) for shape in shapes]
    outs = outs or [VMEM] * len(out)
    one = len(out) == 1

    def call(*args):
        moved = sum(4 * a.size for a in args) + sum(4 * s.size for s in out)
        return pl.pallas_call(
            body,
            out_shape=out[0] if one else out,
            in_specs=ins or [VMEM] * len(args),
            out_specs=outs[0] if one else outs,
            scratch_shapes=scratch,
            input_output_aliases=aliases or {},
            cost_estimate=pl.CostEstimate(flops=flops, bytes_accessed=moved, transcendentals=0),
            compiler_params=pltpu.CompilerParams(vmem_limit_bytes=limit),
        )(*args)

    return call


def swapped(block):
    return lax.ppermute(
        block, "col", [(c, (c + (2 if c % 2 else -2)) % N_COL) for c in range(N_COL)]
    )


def swapped_back(block):
    return lax.ppermute(
        block, "col", [(c, (c + (-2 if c % 2 else 2)) % N_COL) for c in range(N_COL)]
    )


def exchange(pieces, axis):
    n = lax.axis_size(axis)
    rows = pieces.shape[0] // n
    shape = (n, rows, 128) if rows in (4, 8) else (n, 1, rows * 128)
    return lax.all_to_all(pieces.reshape(shape), axis, 0, 0, tiled=True).reshape(pieces.shape)


def on_device(matrix, seats):
    total_rows = matrix.shape[0] * N_ROW
    one = 6 * W**3
    fold_all = local(functools.partial(fold, total_rows), 1, (8 * N_ROW, 128))
    sent = local(
        pack_first,
        one,
        (PIECE * N_ROW, 128),
        ins=[HBM],
        limit=LOAD_LIMIT,
        scratch=[pltpu.VMEM((W, 2 * W), jnp.float32), pltpu.SemaphoreType.DMA((LOADS,))],
    )(matrix)
    tiles = exchange(fold_all(exchange(sent, "row")), "row")
    move = local(first_move, 5 * one, (W, W))(matrix, tiles)
    guest = swapped(move)
    keep, gram, hits = local(
        first_keep, 6 * one, (W, W), (W, W), (4 * N_COL, 128), ins=[VMEM, VMEM, SMEM]
    )(matrix, tiles, seats)
    sent = local(pack_second, 2 * one, (WIDE * N_ROW, 128))(keep, guest, gram)
    folded = local(fold_wide, 1, (WIDE * N_ROW, 128))(exchange(sent, "row"))
    got = exchange(folded, "row")
    new_guest, x, z_keep, z_guest = local(
        functools.partial(second_guest, total_rows), 8 * one, (W, W), (W, W), (W, W), (W, W)
    )(keep, guest, got)
    back = swapped_back(new_guest)
    means, begun = local(
        functools.partial(second_sums, total_rows),
        10 * one,
        (4 * N_COL, 128),
        (W, 2 * W),
        outs=[VMEM, HBM],
        scratch=[pltpu.VMEM((W, W), jnp.float32), pltpu.SemaphoreType.DMA],
    )(x, z_keep, z_guest, got, keep, guest)
    table = exchange(means, "col")
    final, picked = local(
        finish,
        1,
        (W, 2 * W),
        (4, 128),
        ins=[VMEM, VMEM, VMEM, HBM],
        outs=[HBM, HBM],
        scratch=[pltpu.VMEM((4, 128), jnp.float32), pltpu.SemaphoreType.DMA((2,))],
        aliases={3: 0},
    )(hits, back, table, begun)
    return (final, picked.reshape(2 * W))


def solution(mesh):
    placed = (P("row", "col"), P())
    return jax.shard_map(
        on_device,
        mesh=mesh,
        in_specs=placed,
        out_specs=(P("row", "col"), P("col")),
        check_vma=False,
    )
```

```python
import functools

import jax
import jax.numpy as jnp
from jax import lax
from jax.experimental import pallas as pl
from jax.experimental.pallas import tpu as pltpu
from jax.sharding import PartitionSpec as P

W = 256
N_ROW = 64
N_COL = 8
PIECE = 10
WIDE = 17
LOADS = 8
LIMIT = 32 * 1024 * 1024
LOAD_LIMIT = 56000000


def split(a):
    high = a.astype(jnp.bfloat16)
    return high, (a - high.astype(jnp.float32)).astype(jnp.bfloat16)


def product(a, b, ca=1, cb=0):
    def one(p, q):
        return lax.dot_general(
            p, q, (((ca,), (cb,)), ((), ())), preferred_element_type=jnp.float32
        )

    return one(a[0], b[0]) + (one(a[0], b[1]) + one(a[1], b[0]))


def root(s, also):
    parts = split(s)
    s2 = product(parts, parts)
    other = also()
    rows = lax.broadcasted_iota(jnp.int32, s.shape, 0)
    cols = lax.broadcasted_iota(jnp.int32, s.shape, 1)
    eye = jnp.where(rows == cols, 1.0, 0.0).astype(jnp.float32)
    base = eye - 0.5 * s + 0.375 * s2
    return base + product(split(s2), split(0.0625 * s2 - 0.3125 * s)), other


def tile_at(block, r):
    i, half = r % 32, r // 32
    return block[8 * i : 8 * i + 8, 128 * half : 128 * half + 128]


def from_tiles(ref, first, step):
    left = [ref[step * r + first : step * r + first + 8, :] for r in range(32)]
    right = [ref[step * r + first : step * r + first + 8, :] for r in range(32, 64)]
    return jnp.concatenate(
        [jnp.concatenate(left, axis=0), jnp.concatenate(right, axis=0)], axis=1
    )


def roots(*squares):
    parts = [split(s) for s in squares]
    seconds = [product(p, p) for p in parts]
    rows, cols = square_index()
    eye = jnp.where(rows == cols, 1.0, 0.0).astype(jnp.float32)
    return [
        eye - 0.5 * s + 0.375 * s2 + product(split(s2), split(0.0625 * s2 - 0.3125 * s))
        for s, s2 in zip(squares, seconds)
    ]


def column_squares(block):
    return jnp.sum(block * block, axis=0, keepdims=True)


def halves(matrix):
    odd = lax.rem(lax.axis_index("col"), 2)
    keep = matrix[:, pl.ds(pl.multiple_of(odd * W, W), W)]
    move = matrix[:, pl.ds(pl.multiple_of((1 - odd) * W, W), W)]
    return keep, move


def pack_first(whole, out, matrix, arrived):
    rows = W // LOADS
    copies = [
        pltpu.make_async_copy(
            whole.at[pl.ds(k * rows, rows)], matrix.at[pl.ds(k * rows, rows)], arrived.at[k]
        )
        for k in range(LOADS)
    ]
    for copy in copies:
        copy.start()
    for copy in copies:
        copy.wait()
    keep, move = halves(matrix)
    cross = product(split(keep), split(move), 0, 0)
    norm_keep, norm_move = column_squares(keep), column_squares(move)
    for r in range(N_ROW):
        i, half = r % 32, r // 32
        at = PIECE * r
        out[at : at + 8, :] = tile_at(cross, r)
        out[at + 8 : at + 9, :] = norm_keep[:, 128 * (i // 16) : 128 * (i // 16) + 128]
        out[at + 9 : at + 10, :] = norm_move[:, 128 * half : 128 * half + 128]


def square_index():
    rows = lax.broadcasted_iota(jnp.int32, (W, W), 0)
    return rows, lax.broadcasted_iota(jnp.int32, (W, W), 1)


def pack_second(keep, guest, gram_keep, out):
    parts = split(guest[...])
    cross = product(split(keep[...]), parts, 0, 0)
    rows, cols = square_index()
    grams = jnp.where(rows <= cols, gram_keep[...], product(parts, parts, 0, 0))
    norm_guest = column_squares(guest[...])
    for r in range(N_ROW):
        half, at = r // 32, WIDE * r
        out[at : at + 8, :] = tile_at(cross, r)
        out[at + 8 : at + 16, :] = tile_at(grams, r)
        out[at + 16 : at + 17, :] = norm_guest[:, 128 * half : 128 * half + 128]


def fold(total_rows, got, out):
    tile = got[0:8, :]
    norms = got[8:10, :]
    for r in range(1, N_ROW):
        tile += got[PIECE * r : PIECE * r + 8, :]
        norms += got[PIECE * r + 8 : PIECE * r + 10, :]
    sign = jnp.where(lax.rem(lax.axis_index("col"), 2) == 1, -0.5, 0.5)
    first = 8 * lax.rem(lax.axis_index("row"), 16)
    lanes = lax.broadcasted_iota(jnp.int32, (8, 128), 1)
    rows = lax.broadcasted_iota(jnp.int32, (8, 128), 0)
    means = norms / total_rows
    mean_keep = jnp.sum(
        jnp.where(lanes == first + rows, means[0:1], 0.0), axis=1, keepdims=True
    )
    x = sign * (tile / total_rows) / jnp.sqrt((mean_keep + 1e-06) * (means[1:2] + 1e-06))
    for r in range(N_ROW):
        out[8 * r : 8 * r + 8, :] = x


def fold_wide(got, out):
    piece = got[0:WIDE, :]
    for r in range(1, N_ROW):
        piece += got[WIDE * r : WIDE * r + WIDE, :]
    for r in range(N_ROW):
        out[WIDE * r : WIDE * r + WIDE, :] = piece


def first_move(matrix, tiles, out):
    keep, move = halves(matrix)
    x = split(from_tiles(tiles, 0, 8))
    z, mixed = root(product(x, x, 0, 0), lambda: move + product(split(keep), x))
    out[...] = product(split(mixed), split(z))


def first_keep(matrix, tiles, seats, out, gram, hits):
    first = 2 * lax.axis_index("col")
    for k in range(2):
        for seat in range(2 * N_COL):
            at = 2 * N_COL * k + seat
            hit = jnp.where(seats[seat] == first + k, 1.0, 0.0).astype(jnp.float32)
            hits[at : at + 1, :] = jnp.full((1, 128), hit)
    keep, move = halves(matrix)
    x = split(from_tiles(tiles, 0, 8))
    z, mixed = root(product(x, x, 1, 1), lambda: keep - product(split(move), x, 1, 1))
    kept = product(split(mixed), split(z))
    out[...] = kept
    parts = split(kept)
    gram[...] = product(parts, parts, 0, 0)


def guest_squares(got):
    at = 32 * WIDE + 16
    return jnp.concatenate([got[16:17, :], got[at : at + 1, :]], axis=1)


def half_of(ref, odd):
    return ref.at[:, pl.ds(pl.multiple_of(odd * W, W), W)]


def second(total_rows, keep, guest, got, new_guest, sums, final, kept, done):
    crosses = from_tiles(got, 0, WIDE)
    grams = from_tiles(got, 8, WIDE)
    rows, cols = square_index()
    on_diagonal = jnp.where(rows == cols, grams, 0.0)
    mean_keep = jnp.sum(on_diagonal, axis=1, keepdims=True) / total_rows
    mean_guest = guest_squares(got) / total_rows
    sign = jnp.where(lax.rem(lax.axis_index("col"), 2) == 1, -0.5, 0.5) / total_rows
    x = crosses * (sign * lax.rsqrt(mean_keep + 1e-06)) * lax.rsqrt(mean_guest + 1e-06)
    flipped_x = split(x.T)
    x = split(x)
    s_guest = product(flipped_x, flipped_x, 1, 1)
    s_keep = product(x, x, 1, 1)
    old_keep, old_guest = keep[...], guest[...]
    mixed_keep = old_keep - product(split(old_guest), x, 1, 1)
    mixed_guest = old_guest + product(split(old_keep), x)
    z_guest, z = roots(s_guest, s_keep)
    zs, zs_guest = split(z), split(z_guest)
    kept[...] = product(split(mixed_keep), zs)
    odd = lax.rem(lax.axis_index("col"), 2)
    copy = pltpu.make_async_copy(kept, half_of(final, odd), done)
    copy.start()
    new_guest[...] = product(split(mixed_guest), zs_guest)
    cross = split(crosses)
    flipped = grams.T
    of_keep = split(jnp.where(rows <= cols, grams, flipped))
    of_guest = jnp.where(rows > cols, grams, flipped)
    of_guest = split(jnp.where(rows == cols, guest_squares(got), of_guest))
    v = product(flipped_x, zs)
    w = product(x, zs_guest)
    vs, ws = split(v), split(w)
    sum_keep = jnp.sum(
        z * (product(of_keep, zs) - 2.0 * product(cross, vs)) + v * product(of_guest, vs),
        axis=0,
        keepdims=True,
    )
    sum_guest = jnp.sum(
        z_guest * product(of_guest, zs_guest)
        + w * (product(of_keep, ws) + 2.0 * product(cross, zs_guest)),
        axis=0,
        keepdims=True,
    )
    four = [sum_keep[:, :128], sum_keep[:, 128:], sum_guest[:, :128], sum_guest[:, 128:]]
    tile = jnp.maximum(jnp.concatenate(four + four, axis=0) / total_rows, 0.0)
    for r in range(4 * N_COL // 8):
        sums[8 * r : 8 * r + 8, :] = tile
    copy.wait()


def finish(hits, back, table, begun, final, means, picked, done):
    del begun
    col = lax.axis_index("col")
    copy = pltpu.make_async_copy(back, half_of(final, 1 - lax.rem(col, 2)), done.at[0])
    copy.start()
    for k in range(2):
        one = jnp.zeros((2, 128), jnp.float32)
        for c in range(N_COL):
            kept = table[4 * c : 4 * c + 2, :]
            at = 4 * ((c + (2 if c % 2 else -2)) % N_COL) + 2
            hosted = table[at : at + 2, :]
            for b, part in enumerate((hosted, kept) if c % 2 else (kept, hosted)):
                seat = 2 * N_COL * k + 2 * c + b
                one += jnp.where(hits[seat : seat + 1, :] > 0.5, part, 0.0)
        picked[2 * k : 2 * k + 2, :] = one
    means_copy = pltpu.make_async_copy(picked, means, done.at[1])
    means_copy.start()
    copy.wait()
    means_copy.wait()


VMEM = pl.BlockSpec(memory_space=pltpu.VMEM)
SMEM = pl.BlockSpec(memory_space=pltpu.SMEM)
HBM = pl.BlockSpec(memory_space=pltpu.HBM)


def local(body, flops, *shapes, ins=None, outs=None, scratch=(), aliases=None, limit=LIMIT):
    out = [jax.ShapeDtypeStruct(shape, jnp.float32) for shape in shapes]
    outs = outs or [VMEM] * len(out)
    one = len(out) == 1

    def call(*args):
        moved = sum(4 * a.size for a in args) + sum(4 * s.size for s in out)
        return pl.pallas_call(
            body,
            out_shape=out[0] if one else out,
            in_specs=ins or [VMEM] * len(args),
            out_specs=outs[0] if one else outs,
            scratch_shapes=scratch,
            input_output_aliases=aliases or {},
            cost_estimate=pl.CostEstimate(flops=flops, bytes_accessed=moved, transcendentals=0),
            compiler_params=pltpu.CompilerParams(vmem_limit_bytes=limit),
        )(*args)

    return call


def swapped(block):
    return lax.ppermute(
        block, "col", [(c, (c + (2 if c % 2 else -2)) % N_COL) for c in range(N_COL)]
    )


def swapped_back(block):
    return lax.ppermute(
        block, "col", [(c, (c + (-2 if c % 2 else 2)) % N_COL) for c in range(N_COL)]
    )


def exchange(pieces, axis):
    n = lax.axis_size(axis)
    rows = pieces.shape[0] // n
    shape = (n, rows, 128) if rows in (4, 8) else (n, 1, rows * 128)
    return lax.all_to_all(pieces.reshape(shape), axis, 0, 0, tiled=True).reshape(pieces.shape)


def on_device(matrix, seats):
    total_rows = matrix.shape[0] * N_ROW
    one = 6 * W**3
    fold_all = local(functools.partial(fold, total_rows), 1, (8 * N_ROW, 128))
    sent = local(
        pack_first,
        one,
        (PIECE * N_ROW, 128),
        ins=[HBM],
        limit=LOAD_LIMIT,
        scratch=[pltpu.VMEM((W, 2 * W), jnp.float32), pltpu.SemaphoreType.DMA((LOADS,))],
    )(matrix)
    tiles = exchange(fold_all(exchange(sent, "row")), "row")
    move = local(first_move, 5 * one, (W, W))(matrix, tiles)
    guest = swapped(move)
    keep, gram, hits = local(
        first_keep, 6 * one, (W, W), (W, W), (4 * N_COL, 128), ins=[VMEM, VMEM, SMEM]
    )(matrix, tiles, seats)
    sent = local(pack_second, 2 * one, (WIDE * N_ROW, 128))(keep, guest, gram)
    folded = local(fold_wide, 1, (WIDE * N_ROW, 128))(exchange(sent, "row"))
    got = exchange(folded, "row")
    new_guest, means, begun = local(
        functools.partial(second, total_rows),
        18 * one,
        (W, W),
        (4 * N_COL, 128),
        (W, 2 * W),
        outs=[VMEM, VMEM, HBM],
        scratch=[pltpu.VMEM((W, W), jnp.float32), pltpu.SemaphoreType.DMA],
    )(keep, guest, got)
    back = swapped_back(new_guest)
    table = exchange(means, "col")
    final, picked = local(
        finish,
        1,
        (W, 2 * W),
        (4, 128),
        ins=[VMEM, VMEM, VMEM, HBM],
        outs=[HBM, HBM],
        scratch=[pltpu.VMEM((4, 128), jnp.float32), pltpu.SemaphoreType.DMA((2,))],
        aliases={3: 0},
    )(hits, back, table, begun)
    return (final, picked.reshape(2 * W))


def solution(mesh):
    placed = (P("row", "col"), P())
    return jax.shard_map(
        on_device,
        mesh=mesh,
        in_specs=placed,
        out_specs=(P("row", "col"), P("col")),
        check_vma=False,
    )
```

```python
import functools

import jax
import jax.numpy as jnp
from jax import lax
from jax.experimental import pallas as pl
from jax.experimental.pallas import tpu as pltpu
from jax.sharding import Mesh
from jax.sharding import PartitionSpec as P

W = 256
N_ROW = 64
N_COL = 8
ZL, Y, X = 2, 8, 4
PIECE = 10
WIDE_N = 8
WIDE = 136
LOADS = 8
LIMIT = 32 * 1024 * 1024
LOAD_LIMIT = 56000000


def split(a):
    high = a.astype(jnp.bfloat16)
    return high, (a - high.astype(jnp.float32)).astype(jnp.bfloat16)


def product(a, b, ca=1, cb=0):
    def one(p, q):
        return lax.dot_general(
            p, q, (((ca,), (cb,)), ((), ())), preferred_element_type=jnp.float32
        )

    return one(a[0], b[0]) + (one(a[0], b[1]) + one(a[1], b[0]))


def root(s, also):
    parts = split(s)
    s2 = product(parts, parts)
    other = also()
    rows = lax.broadcasted_iota(jnp.int32, s.shape, 0)
    cols = lax.broadcasted_iota(jnp.int32, s.shape, 1)
    eye = jnp.where(rows == cols, 1.0, 0.0).astype(jnp.float32)
    base = eye - 0.5 * s + 0.375 * s2
    return base + product(split(s2), split(0.0625 * s2 - 0.3125 * s)), other


def tile_at(block, r):
    i, half = r % 32, r // 32
    return block[8 * i : 8 * i + 8, 128 * half : 128 * half + 128]


def from_tiles(ref, first, step):
    left = [ref[step * r + first : step * r + first + 8, :] for r in range(32)]
    right = [ref[step * r + first : step * r + first + 8, :] for r in range(32, 64)]
    return jnp.concatenate(
        [jnp.concatenate(left, axis=0), jnp.concatenate(right, axis=0)], axis=1
    )


def roots(*squares):
    parts = [split(s) for s in squares]
    seconds = [product(p, p) for p in parts]
    rows, cols = square_index()
    eye = jnp.where(rows == cols, 1.0, 0.0).astype(jnp.float32)
    return [
        eye - 0.5 * s + 0.375 * s2 + product(split(s2), split(0.0625 * s2 - 0.3125 * s))
        for s, s2 in zip(squares, seconds)
    ]


def column_squares(block):
    return jnp.sum(block * block, axis=0, keepdims=True)


def halves(matrix):
    odd = lax.rem(lax.axis_index("col"), 2)
    keep = matrix[:, pl.ds(pl.multiple_of(odd * W, W), W)]
    move = matrix[:, pl.ds(pl.multiple_of((1 - odd) * W, W), W)]
    return keep, move


def pack_first(whole, out, matrix, arrived):
    rows = W // LOADS
    copies = [
        pltpu.make_async_copy(
            whole.at[pl.ds(k * rows, rows)], matrix.at[pl.ds(k * rows, rows)], arrived.at[k]
        )
        for k in range(LOADS)
    ]
    for copy in copies:
        copy.start()
    for copy in copies:
        copy.wait()
    keep, move = halves(matrix)
    cross = product(split(keep), split(move), 0, 0)
    norm_keep, norm_move = column_squares(keep), column_squares(move)
    for r in range(N_ROW):
        i, half = r % 32, r // 32
        at = PIECE * r
        out[at : at + 8, :] = tile_at(cross, r)
        out[at + 8 : at + 9, :] = norm_keep[:, 128 * (i // 16) : 128 * (i // 16) + 128]
        out[at + 9 : at + 10, :] = norm_move[:, 128 * half : 128 * half + 128]


def square_index():
    rows = lax.broadcasted_iota(jnp.int32, (W, W), 0)
    return rows, lax.broadcasted_iota(jnp.int32, (W, W), 1)


def stacked(block):
    return jnp.concatenate([block[:, :128], block[:, 128:]], axis=0)


def pack_second(keep, guest, gram_keep, out):
    parts = split(guest[...])
    cross = stacked(product(split(keep[...]), parts, 0, 0))
    rows, cols = square_index()
    grams = stacked(jnp.where(rows <= cols, gram_keep[...], product(parts, parts, 0, 0)))
    norms = column_squares(guest[...])
    norms = jnp.concatenate([norms[:, :128], norms[:, 128:]] * 4, axis=0)
    for r in range(WIDE_N):
        at = WIDE * r
        out[at : at + 64, :] = cross[64 * r : 64 * r + 64]
        out[at + 64 : at + 128, :] = grams[64 * r : 64 * r + 64]
        out[at + 128 : at + 136, :] = norms


def fold(total_rows, got, out):
    tile = got[0:8, :]
    norms = got[8:10, :]
    for r in range(1, N_ROW):
        tile += got[PIECE * r : PIECE * r + 8, :]
        norms += got[PIECE * r + 8 : PIECE * r + 10, :]
    sign = jnp.where(lax.rem(lax.axis_index("col"), 2) == 1, -0.5, 0.5)
    first = 8 * lax.rem(lax.axis_index("y") * X + lax.axis_index("x"), 16)
    lanes = lax.broadcasted_iota(jnp.int32, (8, 128), 1)
    rows = lax.broadcasted_iota(jnp.int32, (8, 128), 0)
    means = norms / total_rows
    mean_keep = jnp.sum(
        jnp.where(lanes == first + rows, means[0:1], 0.0), axis=1, keepdims=True
    )
    x = sign * (tile / total_rows) / jnp.sqrt((mean_keep + 1e-06) * (means[1:2] + 1e-06))
    for r in range(N_ROW):
        out[8 * r : 8 * r + 8, :] = x


def fold_wide(got, out):
    piece = got[0:WIDE, :]
    for r in range(1, WIDE_N):
        piece += got[WIDE * r : WIDE * r + WIDE, :]
    for r in range(WIDE_N):
        out[WIDE * r : WIDE * r + WIDE, :] = piece


def from_wide(ref, first):
    at = [WIDE * r + first for r in range(WIDE_N)]
    left = [ref[k : k + 64, :] for k in at[:4]]
    right = [ref[k : k + 64, :] for k in at[4:]]
    return jnp.concatenate(
        [jnp.concatenate(left, axis=0), jnp.concatenate(right, axis=0)], axis=1
    )


def first_move(matrix, tiles, out):
    keep, move = halves(matrix)
    x = split(from_tiles(tiles, 0, 8))
    z, mixed = root(product(x, x, 0, 0), lambda: move + product(split(keep), x))
    out[...] = product(split(mixed), split(z))


def first_keep(matrix, tiles, seats, out, gram, hits):
    first = 2 * lax.axis_index("col")
    for k in range(2):
        for seat in range(2 * N_COL):
            at = 2 * N_COL * k + seat
            hit = jnp.where(seats[seat] == first + k, 1.0, 0.0).astype(jnp.float32)
            hits[at : at + 1, :] = jnp.full((1, 128), hit)
    keep, move = halves(matrix)
    x = split(from_tiles(tiles, 0, 8))
    z, mixed = root(product(x, x, 1, 1), lambda: keep - product(split(move), x, 1, 1))
    kept = product(split(mixed), split(z))
    out[...] = kept
    parts = split(kept)
    gram[...] = product(parts, parts, 0, 0)


def guest_squares(got):
    return jnp.concatenate([got[128:129, :], got[129:130, :]], axis=1)


def half_of(ref, odd):
    return ref.at[:, pl.ds(pl.multiple_of(odd * W, W), W)]


def second(total_rows, keep, guest, got, new_guest, sums, final, kept, done):
    crosses = from_wide(got, 0)
    grams = from_wide(got, 64)
    rows, cols = square_index()
    on_diagonal = jnp.where(rows == cols, grams, 0.0)
    mean_keep = jnp.sum(on_diagonal, axis=1, keepdims=True) / total_rows
    mean_guest = guest_squares(got) / total_rows
    sign = jnp.where(lax.rem(lax.axis_index("col"), 2) == 1, -0.5, 0.5) / total_rows
    x = crosses * (sign * lax.rsqrt(mean_keep + 1e-06)) * lax.rsqrt(mean_guest + 1e-06)
    flipped_x = split(x.T)
    x = split(x)
    s_guest = product(flipped_x, flipped_x, 1, 1)
    s_keep = product(x, x, 1, 1)
    old_keep, old_guest = keep[...], guest[...]
    mixed_keep = old_keep - product(split(old_guest), x, 1, 1)
    mixed_guest = old_guest + product(split(old_keep), x)
    z_guest, z = roots(s_guest, s_keep)
    zs, zs_guest = split(z), split(z_guest)
    kept[...] = product(split(mixed_keep), zs)
    odd = lax.rem(lax.axis_index("col"), 2)
    copy = pltpu.make_async_copy(kept, half_of(final, odd), done)
    copy.start()
    new_guest[...] = product(split(mixed_guest), zs_guest)
    cross = split(crosses)
    flipped = grams.T
    of_keep = split(jnp.where(rows <= cols, grams, flipped))
    of_guest = jnp.where(rows > cols, grams, flipped)
    of_guest = split(jnp.where(rows == cols, guest_squares(got), of_guest))
    v = product(flipped_x, zs)
    w = product(x, zs_guest)
    vs, ws = split(v), split(w)
    sum_keep = jnp.sum(
        z * (product(of_keep, zs) - 2.0 * product(cross, vs)) + v * product(of_guest, vs),
        axis=0,
        keepdims=True,
    )
    sum_guest = jnp.sum(
        z_guest * product(of_guest, zs_guest)
        + w * (product(of_keep, ws) + 2.0 * product(cross, zs_guest)),
        axis=0,
        keepdims=True,
    )
    four = [sum_keep[:, :128], sum_keep[:, 128:], sum_guest[:, :128], sum_guest[:, 128:]]
    tile = jnp.maximum(jnp.concatenate(four + four, axis=0) / total_rows, 0.0)
    for r in range(4 * N_COL // 8):
        sums[8 * r : 8 * r + 8, :] = tile
    copy.wait()


def finish(hits, back, table, begun, final, means, picked, done):
    del begun
    col = lax.axis_index("col")
    copy = pltpu.make_async_copy(back, half_of(final, 1 - lax.rem(col, 2)), done.at[0])
    copy.start()
    for k in range(2):
        one = jnp.zeros((2, 128), jnp.float32)
        for c in range(N_COL):
            kept = table[4 * c : 4 * c + 2, :]
            at = 4 * ((c + (2 if c % 2 else -2)) % N_COL) + 2
            hosted = table[at : at + 2, :]
            for b, part in enumerate((hosted, kept) if c % 2 else (kept, hosted)):
                seat = 2 * N_COL * k + 2 * c + b
                one += jnp.where(hits[seat : seat + 1, :] > 0.5, part, 0.0)
        picked[2 * k : 2 * k + 2, :] = one
    means_copy = pltpu.make_async_copy(picked, means, done.at[1])
    means_copy.start()
    copy.wait()
    means_copy.wait()


VMEM = pl.BlockSpec(memory_space=pltpu.VMEM)
SMEM = pl.BlockSpec(memory_space=pltpu.SMEM)
HBM = pl.BlockSpec(memory_space=pltpu.HBM)


def local(body, flops, *shapes, ins=None, outs=None, scratch=(), aliases=None, limit=LIMIT):
    out = [jax.ShapeDtypeStruct(shape, jnp.float32) for shape in shapes]
    outs = outs or [VMEM] * len(out)
    one = len(out) == 1

    def call(*args):
        moved = sum(4 * a.size for a in args) + sum(4 * s.size for s in out)
        return pl.pallas_call(
            body,
            out_shape=out[0] if one else out,
            in_specs=ins or [VMEM] * len(args),
            out_specs=outs[0] if one else outs,
            scratch_shapes=scratch,
            input_output_aliases=aliases or {},
            cost_estimate=pl.CostEstimate(flops=flops, bytes_accessed=moved, transcendentals=0),
            compiler_params=pltpu.CompilerParams(vmem_limit_bytes=limit),
        )(*args)

    return call


def swapped(block):
    return lax.ppermute(
        block, "col", [(c, (c + (2 if c % 2 else -2)) % N_COL) for c in range(N_COL)]
    )


def swapped_back(block):
    return lax.ppermute(
        block, "col", [(c, (c + (-2 if c % 2 else 2)) % N_COL) for c in range(N_COL)]
    )


ROW = ("zl", "y", "x")


def exchange(pieces, axis):
    n = lax.axis_size(axis)
    rows = pieces.shape[0] // n
    shape = (n, rows, 128) if rows in (4, 8, WIDE) else (n, 1, rows * 128)
    return lax.all_to_all(pieces.reshape(shape), axis, 0, 0, tiled=True).reshape(pieces.shape)


def on_device(matrix, seats):
    total_rows = matrix.shape[0] * N_ROW
    one = 6 * W**3
    fold_all = local(functools.partial(fold, total_rows), 1, (8 * N_ROW, 128))
    sent = local(
        pack_first,
        one,
        (PIECE * N_ROW, 128),
        ins=[HBM],
        limit=LOAD_LIMIT,
        scratch=[pltpu.VMEM((W, 2 * W), jnp.float32), pltpu.SemaphoreType.DMA((LOADS,))],
    )(matrix)
    tiles = exchange(fold_all(exchange(sent, ROW)), ROW)
    move = local(first_move, 5 * one, (W, W))(matrix, tiles)
    guest = swapped(move)
    keep, gram, hits = local(
        first_keep, 6 * one, (W, W), (W, W), (4 * N_COL, 128), ins=[VMEM, VMEM, SMEM]
    )(matrix, tiles, seats)
    sent = local(pack_second, 2 * one, (WIDE * WIDE_N, 128))(keep, guest, gram)
    fold_eight = local(fold_wide, 1, (WIDE * WIDE_N, 128))
    folded = fold_eight(exchange(sent, ("zl", "x")))
    folded = fold_eight(exchange(folded, "y"))
    got = exchange(folded, ("zl", "x"))
    new_guest, means, begun = local(
        functools.partial(second, total_rows),
        18 * one,
        (W, W),
        (4 * N_COL, 128),
        (W, 2 * W),
        outs=[VMEM, VMEM, HBM],
        scratch=[pltpu.VMEM((W, W), jnp.float32), pltpu.SemaphoreType.DMA],
    )(keep, guest, got)
    back = swapped_back(new_guest)
    table = exchange(means, "col")
    final, picked = local(
        finish,
        1,
        (W, 2 * W),
        (4, 128),
        ins=[VMEM, VMEM, VMEM, HBM],
        outs=[HBM, HBM],
        scratch=[pltpu.VMEM((4, 128), jnp.float32), pltpu.SemaphoreType.DMA((2,))],
        aliases={3: 0},
    )(hits, back, table, begun)
    return (final, picked.reshape(2 * W))


def solution(mesh):
    parts = Mesh(mesh.devices.reshape(N_COL, ZL, Y, X), ("col",) + ROW)
    placed = (P(ROW, "col"), P())
    return jax.shard_map(
        on_device,
        mesh=parts,
        in_specs=placed,
        out_specs=(P(ROW, "col"), P("col")),
        check_vma=False,
    )
```

```python
import functools

import jax
import jax.numpy as jnp
from jax import lax
from jax.experimental import pallas as pl
from jax.experimental.pallas import tpu as pltpu
from jax.sharding import Mesh
from jax.sharding import PartitionSpec as P

W = 256
N_ROW = 64
N_COL = 8
ZL, Y, X = 2, 8, 4
EIGHT = 8
NARROW = 72
WIDE = 136
LOADS = 8
LIMIT = 32 * 1024 * 1024
LOAD_LIMIT = 56000000


def split(a):
    high = a.astype(jnp.bfloat16)
    return high, (a - high.astype(jnp.float32)).astype(jnp.bfloat16)


def product(a, b, ca=1, cb=0):
    def one(p, q):
        return lax.dot_general(
            p, q, (((ca,), (cb,)), ((), ())), preferred_element_type=jnp.float32
        )

    return one(a[0], b[0]) + (one(a[0], b[1]) + one(a[1], b[0]))


def root(s, also):
    parts = split(s)
    s2 = product(parts, parts)
    other = also()
    rows = lax.broadcasted_iota(jnp.int32, s.shape, 0)
    cols = lax.broadcasted_iota(jnp.int32, s.shape, 1)
    eye = jnp.where(rows == cols, 1.0, 0.0).astype(jnp.float32)
    base = eye - 0.5 * s + 0.375 * s2
    return base + product(split(s2), split(0.0625 * s2 - 0.3125 * s)), other


def unstacked(ref):
    return jnp.concatenate([ref[:W, :], ref[W:, :]], axis=1)


def roots(*squares):
    parts = [split(s) for s in squares]
    seconds = [product(p, p) for p in parts]
    rows, cols = square_index()
    eye = jnp.where(rows == cols, 1.0, 0.0).astype(jnp.float32)
    return [
        eye - 0.5 * s + 0.375 * s2 + product(split(s2), split(0.0625 * s2 - 0.3125 * s))
        for s, s2 in zip(squares, seconds)
    ]


def column_squares(block):
    return jnp.sum(block * block, axis=0, keepdims=True)


def halves(matrix):
    odd = lax.rem(lax.axis_index("col"), 2)
    keep = matrix[:, pl.ds(pl.multiple_of(odd * W, W), W)]
    move = matrix[:, pl.ds(pl.multiple_of((1 - odd) * W, W), W)]
    return keep, move


def pack_first(whole, out, matrix, arrived):
    rows = W // LOADS
    copies = [
        pltpu.make_async_copy(
            whole.at[pl.ds(k * rows, rows)], matrix.at[pl.ds(k * rows, rows)], arrived.at[k]
        )
        for k in range(LOADS)
    ]
    for copy in copies:
        copy.start()
    for copy in copies:
        copy.wait()
    keep, move = halves(matrix)
    cross = stacked(product(split(keep), split(move), 0, 0))
    norm_keep, norm_move = column_squares(keep), column_squares(move)
    for r in range(EIGHT):
        at = NARROW * r
        out[at : at + 64, :] = cross[64 * r : 64 * r + 64]
        half = (r % 4) // 2
        pair = [norm_keep[:, 128 * half : 128 * half + 128]]
        pair.append(norm_move[:, 128 * (r // 4) : 128 * (r // 4) + 128])
        out[at + 64 : at + 72, :] = jnp.concatenate(pair * 4, axis=0)


def square_index():
    rows = lax.broadcasted_iota(jnp.int32, (W, W), 0)
    return rows, lax.broadcasted_iota(jnp.int32, (W, W), 1)


def stacked(block):
    return jnp.concatenate([block[:, :128], block[:, 128:]], axis=0)


def pack_second(keep, guest, gram_keep, out):
    parts = split(guest[...])
    cross = stacked(product(split(keep[...]), parts, 0, 0))
    rows, cols = square_index()
    grams = stacked(jnp.where(rows <= cols, gram_keep[...], product(parts, parts, 0, 0)))
    norms = column_squares(guest[...])
    norms = jnp.concatenate([norms[:, :128], norms[:, 128:]] * 4, axis=0)
    for r in range(EIGHT):
        at = WIDE * r
        out[at : at + 64, :] = cross[64 * r : 64 * r + 64]
        out[at + 64 : at + 128, :] = grams[64 * r : 64 * r + 64]
        out[at + 128 : at + 136, :] = norms


def added(got, size):
    piece = got[0:size, :]
    for r in range(1, EIGHT):
        piece += got[size * r : size * r + size, :]
    return piece


def fold(size, got, out):
    piece = added(got, size)
    for r in range(EIGHT):
        out[size * r : size * r + size, :] = piece


def fold_first(total_rows, got, out):
    piece = added(got, NARROW) / total_rows
    sign = jnp.where(lax.rem(lax.axis_index("col"), 2) == 1, -0.5, 0.5)
    first = 64 * lax.rem(lax.axis_index("x"), 2)
    lanes = lax.broadcasted_iota(jnp.int32, (64, 128), 1)
    rows = lax.broadcasted_iota(jnp.int32, (64, 128), 0)
    mean_keep = jnp.sum(
        jnp.where(lanes == first + rows, piece[64:65], 0.0), axis=1, keepdims=True
    )
    x = sign * piece[:64] / jnp.sqrt((mean_keep + 1e-06) * (piece[65:66] + 1e-06))
    for r in range(EIGHT):
        out[64 * r : 64 * r + 64, :] = x


def from_wide(ref, first):
    at = [WIDE * r + first for r in range(EIGHT)]
    left = [ref[k : k + 64, :] for k in at[:4]]
    right = [ref[k : k + 64, :] for k in at[4:]]
    return jnp.concatenate(
        [jnp.concatenate(left, axis=0), jnp.concatenate(right, axis=0)], axis=1
    )


def first_move(matrix, tiles, out):
    keep, move = halves(matrix)
    x = split(unstacked(tiles))
    z, mixed = root(product(x, x, 0, 0), lambda: move + product(split(keep), x))
    out[...] = product(split(mixed), split(z))


def first_keep(matrix, tiles, seats, out, gram, hits):
    first = 2 * lax.axis_index("col")
    for k in range(2):
        for seat in range(2 * N_COL):
            at = 2 * N_COL * k + seat
            hit = jnp.where(seats[seat] == first + k, 1.0, 0.0).astype(jnp.float32)
            hits[at : at + 1, :] = jnp.full((1, 128), hit)
    keep, move = halves(matrix)
    x = split(unstacked(tiles))
    z, mixed = root(product(x, x, 1, 1), lambda: keep - product(split(move), x, 1, 1))
    kept = product(split(mixed), split(z))
    out[...] = kept
    parts = split(kept)
    gram[...] = product(parts, parts, 0, 0)


def guest_squares(got):
    return jnp.concatenate([got[128:129, :], got[129:130, :]], axis=1)


def half_of(ref, odd):
    return ref.at[:, pl.ds(pl.multiple_of(odd * W, W), W)]


def second(total_rows, keep, guest, got, new_guest, sums, final, kept, done):
    crosses = from_wide(got, 0)
    grams = from_wide(got, 64)
    rows, cols = square_index()
    on_diagonal = jnp.where(rows == cols, grams, 0.0)
    mean_keep = jnp.sum(on_diagonal, axis=1, keepdims=True) / total_rows
    mean_guest = guest_squares(got) / total_rows
    sign = jnp.where(lax.rem(lax.axis_index("col"), 2) == 1, -0.5, 0.5) / total_rows
    x = crosses * (sign * lax.rsqrt(mean_keep + 1e-06)) * lax.rsqrt(mean_guest + 1e-06)
    flipped_x = split(x.T)
    x = split(x)
    s_guest = product(flipped_x, flipped_x, 1, 1)
    s_keep = product(x, x, 1, 1)
    old_keep, old_guest = keep[...], guest[...]
    mixed_keep = old_keep - product(split(old_guest), x, 1, 1)
    mixed_guest = old_guest + product(split(old_keep), x)
    z_guest, z = roots(s_guest, s_keep)
    zs, zs_guest = split(z), split(z_guest)
    kept[...] = product(split(mixed_keep), zs)
    odd = lax.rem(lax.axis_index("col"), 2)
    copy = pltpu.make_async_copy(kept, half_of(final, odd), done)
    copy.start()
    new_guest[...] = product(split(mixed_guest), zs_guest)
    cross = split(crosses)
    flipped = grams.T
    of_keep = split(jnp.where(rows <= cols, grams, flipped))
    of_guest = jnp.where(rows > cols, grams, flipped)
    of_guest = split(jnp.where(rows == cols, guest_squares(got), of_guest))
    v = product(flipped_x, zs)
    w = product(x, zs_guest)
    vs, ws = split(v), split(w)
    sum_keep = jnp.sum(
        z * (product(of_keep, zs) - 2.0 * product(cross, vs)) + v * product(of_guest, vs),
        axis=0,
        keepdims=True,
    )
    sum_guest = jnp.sum(
        z_guest * product(of_guest, zs_guest)
        + w * (product(of_keep, ws) + 2.0 * product(cross, zs_guest)),
        axis=0,
        keepdims=True,
    )
    four = [sum_keep[:, :128], sum_keep[:, 128:], sum_guest[:, :128], sum_guest[:, 128:]]
    tile = jnp.maximum(jnp.concatenate(four + four, axis=0) / total_rows, 0.0)
    for r in range(4 * N_COL // 8):
        sums[8 * r : 8 * r + 8, :] = tile
    copy.wait()


def finish(hits, back, table, begun, final, means, picked, done):
    del begun
    col = lax.axis_index("col")
    copy = pltpu.make_async_copy(back, half_of(final, 1 - lax.rem(col, 2)), done.at[0])
    copy.start()
    for k in range(2):
        one = jnp.zeros((2, 128), jnp.float32)
        for c in range(N_COL):
            kept = table[4 * c : 4 * c + 2, :]
            at = 4 * ((c + (2 if c % 2 else -2)) % N_COL) + 2
            hosted = table[at : at + 2, :]
            for b, part in enumerate((hosted, kept) if c % 2 else (kept, hosted)):
                seat = 2 * N_COL * k + 2 * c + b
                one += jnp.where(hits[seat : seat + 1, :] > 0.5, part, 0.0)
        picked[2 * k : 2 * k + 2, :] = one
    means_copy = pltpu.make_async_copy(picked, means, done.at[1])
    means_copy.start()
    copy.wait()
    means_copy.wait()


VMEM = pl.BlockSpec(memory_space=pltpu.VMEM)
SMEM = pl.BlockSpec(memory_space=pltpu.SMEM)
HBM = pl.BlockSpec(memory_space=pltpu.HBM)


def local(body, flops, *shapes, ins=None, outs=None, scratch=(), aliases=None, limit=LIMIT):
    out = [jax.ShapeDtypeStruct(shape, jnp.float32) for shape in shapes]
    outs = outs or [VMEM] * len(out)
    one = len(out) == 1

    def call(*args):
        moved = sum(4 * a.size for a in args) + sum(4 * s.size for s in out)
        return pl.pallas_call(
            body,
            out_shape=out[0] if one else out,
            in_specs=ins or [VMEM] * len(args),
            out_specs=outs[0] if one else outs,
            scratch_shapes=scratch,
            input_output_aliases=aliases or {},
            cost_estimate=pl.CostEstimate(flops=flops, bytes_accessed=moved, transcendentals=0),
            compiler_params=pltpu.CompilerParams(vmem_limit_bytes=limit),
        )(*args)

    return call


def swapped(block):
    return lax.ppermute(
        block, "col", [(c, (c + (2 if c % 2 else -2)) % N_COL) for c in range(N_COL)]
    )


def swapped_back(block):
    return lax.ppermute(
        block, "col", [(c, (c + (-2 if c % 2 else 2)) % N_COL) for c in range(N_COL)]
    )


ROW = ("zl", "y", "x")


def exchange(pieces, axis):
    split_up = pieces.reshape(lax.axis_size(axis), -1, 128)
    return lax.all_to_all(split_up, axis, 0, 0, tiled=True).reshape(pieces.shape)


def on_device(matrix, seats):
    total_rows = matrix.shape[0] * N_ROW
    one = 6 * W**3
    sent = local(
        pack_first,
        one,
        (NARROW * EIGHT, 128),
        ins=[HBM],
        limit=LOAD_LIMIT,
        scratch=[pltpu.VMEM((W, 2 * W), jnp.float32), pltpu.SemaphoreType.DMA((LOADS,))],
    )(matrix)
    folded = local(functools.partial(fold, NARROW), 1, (NARROW * EIGHT, 128))(
        exchange(sent, ("zl", "x"))
    )
    tiles = local(functools.partial(fold_first, total_rows), 1, (64 * EIGHT, 128))(
        exchange(folded, "y")
    )
    tiles = exchange(tiles, ("zl", "x"))
    move = local(first_move, 5 * one, (W, W))(matrix, tiles)
    guest = swapped(move)
    keep, gram, hits = local(
        first_keep, 6 * one, (W, W), (W, W), (4 * N_COL, 128), ins=[VMEM, VMEM, SMEM]
    )(matrix, tiles, seats)
    sent = local(pack_second, 2 * one, (WIDE * EIGHT, 128))(keep, guest, gram)
    fold_eight = local(functools.partial(fold, WIDE), 1, (WIDE * EIGHT, 128))
    folded = fold_eight(exchange(sent, ("zl", "x")))
    folded = fold_eight(exchange(folded, "y"))
    got = exchange(folded, ("zl", "x"))
    new_guest, means, begun = local(
        functools.partial(second, total_rows),
        18 * one,
        (W, W),
        (4 * N_COL, 128),
        (W, 2 * W),
        outs=[VMEM, VMEM, HBM],
        scratch=[pltpu.VMEM((W, W), jnp.float32), pltpu.SemaphoreType.DMA],
    )(keep, guest, got)
    back = swapped_back(new_guest)
    table = exchange(means, "col")
    final, picked = local(
        finish,
        1,
        (W, 2 * W),
        (4, 128),
        ins=[VMEM, VMEM, VMEM, HBM],
        outs=[HBM, HBM],
        scratch=[pltpu.VMEM((4, 128), jnp.float32), pltpu.SemaphoreType.DMA((2,))],
        aliases={3: 0},
    )(hits, back, table, begun)
    return (final, picked.reshape(2 * W))


def solution(mesh):
    parts = Mesh(mesh.devices.reshape(N_COL, ZL, Y, X), ("col",) + ROW)
    placed = (P(ROW, "col"), P())
    return jax.shard_map(
        on_device,
        mesh=parts,
        in_specs=placed,
        out_specs=(P(ROW, "col"), P("col")),
        check_vma=False,
    )
```

```python
import functools

import jax
import jax.numpy as jnp
from jax import lax
from jax.experimental import pallas as pl
from jax.experimental.pallas import tpu as pltpu
from jax.sharding import Mesh
from jax.sharding import PartitionSpec as P

W = 256
N_ROW = 64
N_COL = 8
ZL, Y, X = 2, 8, 4
EIGHT = 8
NARROW = 66
WIDE = 129
LOADS = 8
LIMIT = 32 * 1024 * 1024
LOAD_LIMIT = 56000000


def split(a):
    high = a.astype(jnp.bfloat16)
    return high, (a - high.astype(jnp.float32)).astype(jnp.bfloat16)


def product(a, b, ca=1, cb=0):
    def one(p, q):
        return lax.dot_general(
            p, q, (((ca,), (cb,)), ((), ())), preferred_element_type=jnp.float32
        )

    return one(a[0], b[0]) + (one(a[0], b[1]) + one(a[1], b[0]))


def root(s, also):
    parts = split(s)
    s2 = product(parts, parts)
    other = also()
    rows = lax.broadcasted_iota(jnp.int32, s.shape, 0)
    cols = lax.broadcasted_iota(jnp.int32, s.shape, 1)
    eye = jnp.where(rows == cols, 1.0, 0.0).astype(jnp.float32)
    base = eye - 0.5 * s + 0.375 * s2
    return base + product(split(s2), split(0.0625 * s2 - 0.3125 * s)), other


def unstacked(ref):
    return jnp.concatenate([ref[:W, :], ref[W:, :]], axis=1)


def roots(*squares):
    parts = [split(s) for s in squares]
    seconds = [product(p, p) for p in parts]
    rows, cols = square_index()
    eye = jnp.where(rows == cols, 1.0, 0.0).astype(jnp.float32)
    return [
        eye - 0.5 * s + 0.375 * s2 + product(split(s2), split(0.0625 * s2 - 0.3125 * s))
        for s, s2 in zip(squares, seconds)
    ]


def column_squares(block):
    return jnp.sum(block * block, axis=0, keepdims=True)


def halves(matrix):
    odd = lax.rem(lax.axis_index("col"), 2)
    keep = matrix[:, pl.ds(pl.multiple_of(odd * W, W), W)]
    move = matrix[:, pl.ds(pl.multiple_of((1 - odd) * W, W), W)]
    return keep, move


def pack_first(whole, out, matrix, arrived):
    rows = W // LOADS
    copies = [
        pltpu.make_async_copy(
            whole.at[pl.ds(k * rows, rows)], matrix.at[pl.ds(k * rows, rows)], arrived.at[k]
        )
        for k in range(LOADS)
    ]
    for copy in copies:
        copy.start()
    for copy in copies:
        copy.wait()
    keep, move = halves(matrix)
    cross = stacked(product(split(keep), split(move), 0, 0))
    norm_keep, norm_move = column_squares(keep), column_squares(move)
    for r in range(EIGHT):
        at = NARROW * r
        out[at : at + 64, :] = cross[64 * r : 64 * r + 64]
        half = (r % 4) // 2
        out[at + 64 : at + 65, :] = norm_keep[:, 128 * half : 128 * half + 128]
        out[at + 65 : at + 66, :] = norm_move[:, 128 * (r // 4) : 128 * (r // 4) + 128]


def square_index():
    rows = lax.broadcasted_iota(jnp.int32, (W, W), 0)
    return rows, lax.broadcasted_iota(jnp.int32, (W, W), 1)


def stacked(block):
    return jnp.concatenate([block[:, :128], block[:, 128:]], axis=0)


def pack_second(keep, guest, gram_keep, out):
    parts = split(guest[...])
    cross = stacked(product(split(keep[...]), parts, 0, 0))
    rows, cols = square_index()
    grams = stacked(jnp.where(rows <= cols, gram_keep[...], product(parts, parts, 0, 0)))
    norms = column_squares(guest[...])
    for r in range(EIGHT):
        at = WIDE * r
        out[at : at + 64, :] = cross[64 * r : 64 * r + 64]
        out[at + 64 : at + 128, :] = grams[64 * r : 64 * r + 64]
        out[at + 128 : at + 129, :] = norms[:, 128 * (r // 4) : 128 * (r // 4) + 128]


def added(got, size):
    piece = got[0:size, :]
    for r in range(1, EIGHT):
        piece += got[size * r : size * r + size, :]
    return piece


def fold(size, got, out):
    piece = added(got, size)
    for r in range(EIGHT):
        out[size * r : size * r + size, :] = piece


def fold_first(total_rows, got, out):
    piece = added(got, NARROW) / total_rows
    sign = jnp.where(lax.rem(lax.axis_index("col"), 2) == 1, -0.5, 0.5)
    first = 64 * lax.rem(lax.axis_index("x"), 2)
    lanes = lax.broadcasted_iota(jnp.int32, (64, 128), 1)
    rows = lax.broadcasted_iota(jnp.int32, (64, 128), 0)
    mean_keep = jnp.sum(
        jnp.where(lanes == first + rows, piece[64:65], 0.0), axis=1, keepdims=True
    )
    x = sign * piece[:64] / jnp.sqrt((mean_keep + 1e-06) * (piece[65:66] + 1e-06))
    for r in range(EIGHT):
        out[64 * r : 64 * r + 64, :] = x


def from_wide(ref, first):
    at = [WIDE * r + first for r in range(EIGHT)]
    left = [ref[k : k + 64, :] for k in at[:4]]
    right = [ref[k : k + 64, :] for k in at[4:]]
    return jnp.concatenate(
        [jnp.concatenate(left, axis=0), jnp.concatenate(right, axis=0)], axis=1
    )


def first_move(matrix, tiles, out):
    keep, move = halves(matrix)
    x = split(unstacked(tiles))
    z, mixed = root(product(x, x, 0, 0), lambda: move + product(split(keep), x))
    out[...] = product(split(mixed), split(z))


def first_keep(matrix, tiles, seats, out, gram, hits):
    first = 2 * lax.axis_index("col")
    for k in range(2):
        for seat in range(2 * N_COL):
            at = 2 * N_COL * k + seat
            hit = jnp.where(seats[seat] == first + k, 1.0, 0.0).astype(jnp.float32)
            hits[at : at + 1, :] = jnp.full((1, 128), hit)
    keep, move = halves(matrix)
    x = split(unstacked(tiles))
    z, mixed = root(product(x, x, 1, 1), lambda: keep - product(split(move), x, 1, 1))
    kept = product(split(mixed), split(z))
    out[...] = kept
    parts = split(kept)
    gram[...] = product(parts, parts, 0, 0)


def guest_squares(got):
    at = 4 * WIDE + 128
    return jnp.concatenate([got[128:129, :], got[at : at + 1, :]], axis=1)


def half_of(ref, odd):
    return ref.at[:, pl.ds(pl.multiple_of(odd * W, W), W)]


def second(total_rows, keep, guest, got, new_guest, sums, final, kept, done):
    crosses = from_wide(got, 0)
    grams = from_wide(got, 64)
    rows, cols = square_index()
    on_diagonal = jnp.where(rows == cols, grams, 0.0)
    mean_keep = jnp.sum(on_diagonal, axis=1, keepdims=True) / total_rows
    mean_guest = guest_squares(got) / total_rows
    sign = jnp.where(lax.rem(lax.axis_index("col"), 2) == 1, -0.5, 0.5) / total_rows
    x = crosses * (sign * lax.rsqrt(mean_keep + 1e-06)) * lax.rsqrt(mean_guest + 1e-06)
    flipped_x = split(x.T)
    x = split(x)
    s_guest = product(flipped_x, flipped_x, 1, 1)
    s_keep = product(x, x, 1, 1)
    old_keep, old_guest = keep[...], guest[...]
    mixed_keep = old_keep - product(split(old_guest), x, 1, 1)
    mixed_guest = old_guest + product(split(old_keep), x)
    z_guest, z = roots(s_guest, s_keep)
    zs, zs_guest = split(z), split(z_guest)
    kept[...] = product(split(mixed_keep), zs)
    odd = lax.rem(lax.axis_index("col"), 2)
    copy = pltpu.make_async_copy(kept, half_of(final, odd), done)
    copy.start()
    new_guest[...] = product(split(mixed_guest), zs_guest)
    cross = split(crosses)
    flipped = grams.T
    of_keep = split(jnp.where(rows <= cols, grams, flipped))
    of_guest = jnp.where(rows > cols, grams, flipped)
    of_guest = split(jnp.where(rows == cols, guest_squares(got), of_guest))
    v = product(flipped_x, zs)
    w = product(x, zs_guest)
    vs, ws = split(v), split(w)
    sum_keep = jnp.sum(
        z * (product(of_keep, zs) - 2.0 * product(cross, vs)) + v * product(of_guest, vs),
        axis=0,
        keepdims=True,
    )
    sum_guest = jnp.sum(
        z_guest * product(of_guest, zs_guest)
        + w * (product(of_keep, ws) + 2.0 * product(cross, zs_guest)),
        axis=0,
        keepdims=True,
    )
    four = [sum_keep[:, :128], sum_keep[:, 128:], sum_guest[:, :128], sum_guest[:, 128:]]
    tile = jnp.maximum(jnp.concatenate(four + four, axis=0) / total_rows, 0.0)
    for r in range(4 * N_COL // 8):
        sums[8 * r : 8 * r + 8, :] = tile
    copy.wait()


def finish(hits, back, table, begun, final, means, picked, done):
    del begun
    col = lax.axis_index("col")
    copy = pltpu.make_async_copy(back, half_of(final, 1 - lax.rem(col, 2)), done.at[0])
    copy.start()
    for k in range(2):
        one = jnp.zeros((2, 128), jnp.float32)
        for c in range(N_COL):
            kept = table[4 * c : 4 * c + 2, :]
            at = 4 * ((c + (2 if c % 2 else -2)) % N_COL) + 2
            hosted = table[at : at + 2, :]
            for b, part in enumerate((hosted, kept) if c % 2 else (kept, hosted)):
                seat = 2 * N_COL * k + 2 * c + b
                one += jnp.where(hits[seat : seat + 1, :] > 0.5, part, 0.0)
        picked[2 * k : 2 * k + 2, :] = one
    means_copy = pltpu.make_async_copy(picked, means, done.at[1])
    means_copy.start()
    copy.wait()
    means_copy.wait()


VMEM = pl.BlockSpec(memory_space=pltpu.VMEM)
SMEM = pl.BlockSpec(memory_space=pltpu.SMEM)
HBM = pl.BlockSpec(memory_space=pltpu.HBM)


def local(body, flops, *shapes, ins=None, outs=None, scratch=(), aliases=None, limit=LIMIT):
    out = [jax.ShapeDtypeStruct(shape, jnp.float32) for shape in shapes]
    outs = outs or [VMEM] * len(out)
    one = len(out) == 1

    def call(*args):
        moved = sum(4 * a.size for a in args) + sum(4 * s.size for s in out)
        return pl.pallas_call(
            body,
            out_shape=out[0] if one else out,
            in_specs=ins or [VMEM] * len(args),
            out_specs=outs[0] if one else outs,
            scratch_shapes=scratch,
            input_output_aliases=aliases or {},
            cost_estimate=pl.CostEstimate(flops=flops, bytes_accessed=moved, transcendentals=0),
            compiler_params=pltpu.CompilerParams(vmem_limit_bytes=limit),
        )(*args)

    return call


def swapped(block):
    return lax.ppermute(
        block, "col", [(c, (c + (2 if c % 2 else -2)) % N_COL) for c in range(N_COL)]
    )


def swapped_back(block):
    return lax.ppermute(
        block, "col", [(c, (c + (-2 if c % 2 else 2)) % N_COL) for c in range(N_COL)]
    )


ROW = ("zl", "y", "x")


def exchange(pieces, axis):
    n = lax.axis_size(axis)
    rows = pieces.shape[0] // n
    shape = (n, rows, 128) if rows % 4 == 0 else (n, 1, rows * 128)
    split_up = pieces.reshape(shape)
    return lax.all_to_all(split_up, axis, 0, 0, tiled=True).reshape(pieces.shape)


def on_device(matrix, seats):
    total_rows = matrix.shape[0] * N_ROW
    one = 6 * W**3
    sent = local(
        pack_first,
        one,
        (NARROW * EIGHT, 128),
        ins=[HBM],
        limit=LOAD_LIMIT,
        scratch=[pltpu.VMEM((W, 2 * W), jnp.float32), pltpu.SemaphoreType.DMA((LOADS,))],
    )(matrix)
    folded = local(functools.partial(fold, NARROW), 1, (NARROW * EIGHT, 128))(
        exchange(sent, ("zl", "x"))
    )
    tiles = local(functools.partial(fold_first, total_rows), 1, (64 * EIGHT, 128))(
        exchange(folded, "y")
    )
    tiles = exchange(tiles, ("zl", "x"))
    move = local(first_move, 5 * one, (W, W))(matrix, tiles)
    guest = swapped(move)
    keep, gram, hits = local(
        first_keep, 6 * one, (W, W), (W, W), (4 * N_COL, 128), ins=[VMEM, VMEM, SMEM]
    )(matrix, tiles, seats)
    sent = local(pack_second, 2 * one, (WIDE * EIGHT, 128))(keep, guest, gram)
    fold_eight = local(functools.partial(fold, WIDE), 1, (WIDE * EIGHT, 128))
    folded = fold_eight(exchange(sent, ("zl", "x")))
    folded = fold_eight(exchange(folded, "y"))
    got = exchange(folded, ("zl", "x"))
    new_guest, means, begun = local(
        functools.partial(second, total_rows),
        18 * one,
        (W, W),
        (4 * N_COL, 128),
        (W, 2 * W),
        outs=[VMEM, VMEM, HBM],
        scratch=[pltpu.VMEM((W, W), jnp.float32), pltpu.SemaphoreType.DMA],
    )(keep, guest, got)
    back = swapped_back(new_guest)
    table = exchange(means, "col")
    final, picked = local(
        finish,
        1,
        (W, 2 * W),
        (4, 128),
        ins=[VMEM, VMEM, VMEM, HBM],
        outs=[HBM, HBM],
        scratch=[pltpu.VMEM((4, 128), jnp.float32), pltpu.SemaphoreType.DMA((2,))],
        aliases={3: 0},
    )(hits, back, table, begun)
    return (final, picked.reshape(2 * W))


def solution(mesh):
    parts = Mesh(mesh.devices.reshape(N_COL, ZL, Y, X), ("col",) + ROW)
    placed = (P(ROW, "col"), P())
    return jax.shard_map(
        on_device,
        mesh=parts,
        in_specs=placed,
        out_specs=(P(ROW, "col"), P("col")),
        check_vma=False,
    )
```

```python
import functools

import jax
import jax.numpy as jnp
from jax import lax
from jax.experimental import pallas as pl
from jax.experimental.pallas import tpu as pltpu
from jax.sharding import Mesh
from jax.sharding import PartitionSpec as P

W = 256
N_ROW = 64
N_COL = 8
ROW_PARTS = (2, 4, 2, 4)
EIGHT = 8
NARROW = 66
WIDE = 129
LOADS = 8
LIMIT = 32 * 1024 * 1024
LOAD_LIMIT = 56000000


def split(a):
    high = a.astype(jnp.bfloat16)
    return high, (a - high.astype(jnp.float32)).astype(jnp.bfloat16)


def product(a, b, ca=1, cb=0):
    def one(p, q):
        return lax.dot_general(
            p, q, (((ca,), (cb,)), ((), ())), preferred_element_type=jnp.float32
        )

    return one(a[0], b[0]) + (one(a[0], b[1]) + one(a[1], b[0]))


def root(s, also):
    parts = split(s)
    s2 = product(parts, parts)
    other = also()
    rows = lax.broadcasted_iota(jnp.int32, s.shape, 0)
    cols = lax.broadcasted_iota(jnp.int32, s.shape, 1)
    eye = jnp.where(rows == cols, 1.0, 0.0).astype(jnp.float32)
    base = eye - 0.5 * s + 0.375 * s2
    return base + product(split(s2), split(0.0625 * s2 - 0.3125 * s)), other


def unstacked(ref):
    return jnp.concatenate([ref[:W, :], ref[W:, :]], axis=1)


def roots(*squares):
    parts = [split(s) for s in squares]
    seconds = [product(p, p) for p in parts]
    rows, cols = square_index()
    eye = jnp.where(rows == cols, 1.0, 0.0).astype(jnp.float32)
    return [
        eye - 0.5 * s + 0.375 * s2 + product(split(s2), split(0.0625 * s2 - 0.3125 * s))
        for s, s2 in zip(squares, seconds)
    ]


def column_squares(block):
    return jnp.sum(block * block, axis=0, keepdims=True)


def halves(matrix):
    odd = lax.rem(lax.axis_index("col"), 2)
    keep = matrix[:, pl.ds(pl.multiple_of(odd * W, W), W)]
    move = matrix[:, pl.ds(pl.multiple_of((1 - odd) * W, W), W)]
    return keep, move


def pack_first(whole, out, matrix, arrived):
    rows = W // LOADS
    copies = [
        pltpu.make_async_copy(
            whole.at[pl.ds(k * rows, rows)], matrix.at[pl.ds(k * rows, rows)], arrived.at[k]
        )
        for k in range(LOADS)
    ]
    for copy in copies:
        copy.start()
    for copy in copies:
        copy.wait()
    keep, move = halves(matrix)
    cross = stacked(product(split(keep), split(move), 0, 0))
    norm_keep, norm_move = column_squares(keep), column_squares(move)
    for r in range(EIGHT):
        at = NARROW * r
        out[at : at + 64, :] = cross[64 * r : 64 * r + 64]
        half = (r % 4) // 2
        out[at + 64 : at + 65, :] = norm_keep[:, 128 * half : 128 * half + 128]
        out[at + 65 : at + 66, :] = norm_move[:, 128 * (r // 4) : 128 * (r // 4) + 128]


def square_index():
    rows = lax.broadcasted_iota(jnp.int32, (W, W), 0)
    return rows, lax.broadcasted_iota(jnp.int32, (W, W), 1)


def stacked(block):
    return jnp.concatenate([block[:, :128], block[:, 128:]], axis=0)


def pack_second(keep, guest, gram_keep, out):
    parts = split(guest[...])
    cross = stacked(product(split(keep[...]), parts, 0, 0))
    rows, cols = square_index()
    grams = stacked(jnp.where(rows <= cols, gram_keep[...], product(parts, parts, 0, 0)))
    norms = column_squares(guest[...])
    for r in range(EIGHT):
        at = WIDE * r
        out[at : at + 64, :] = cross[64 * r : 64 * r + 64]
        out[at + 64 : at + 128, :] = grams[64 * r : 64 * r + 64]
        out[at + 128 : at + 129, :] = norms[:, 128 * (r // 4) : 128 * (r // 4) + 128]


def added(got, size):
    piece = got[0:size, :]
    for r in range(1, EIGHT):
        piece += got[size * r : size * r + size, :]
    return piece


def fold(size, got, out):
    piece = added(got, size)
    for r in range(EIGHT):
        out[size * r : size * r + size, :] = piece


def fold_first(total_rows, got, out):
    piece = added(got, NARROW) / total_rows
    sign = jnp.where(lax.rem(lax.axis_index("col"), 2) == 1, -0.5, 0.5)
    first = 64 * lax.rem(lax.axis_index("x"), 2)
    lanes = lax.broadcasted_iota(jnp.int32, (64, 128), 1)
    rows = lax.broadcasted_iota(jnp.int32, (64, 128), 0)
    mean_keep = jnp.sum(
        jnp.where(lanes == first + rows, piece[64:65], 0.0), axis=1, keepdims=True
    )
    x = sign * piece[:64] / jnp.sqrt((mean_keep + 1e-06) * (piece[65:66] + 1e-06))
    for r in range(EIGHT):
        out[64 * r : 64 * r + 64, :] = x


def from_wide(ref, first):
    at = [WIDE * r + first for r in range(EIGHT)]
    left = [ref[k : k + 64, :] for k in at[:4]]
    right = [ref[k : k + 64, :] for k in at[4:]]
    return jnp.concatenate(
        [jnp.concatenate(left, axis=0), jnp.concatenate(right, axis=0)], axis=1
    )


def first_move(matrix, tiles, out):
    keep, move = halves(matrix)
    x = split(unstacked(tiles))
    z, mixed = root(product(x, x, 0, 0), lambda: move + product(split(keep), x))
    out[...] = product(split(mixed), split(z))


def first_keep(matrix, tiles, seats, out, gram, hits):
    first = 2 * lax.axis_index("col")
    for k in range(2):
        for seat in range(2 * N_COL):
            at = 2 * N_COL * k + seat
            hit = jnp.where(seats[seat] == first + k, 1.0, 0.0).astype(jnp.float32)
            hits[at : at + 1, :] = jnp.full((1, 128), hit)
    keep, move = halves(matrix)
    x = split(unstacked(tiles))
    z, mixed = root(product(x, x, 1, 1), lambda: keep - product(split(move), x, 1, 1))
    kept = product(split(mixed), split(z))
    out[...] = kept
    parts = split(kept)
    gram[...] = product(parts, parts, 0, 0)


def guest_squares(got):
    at = 4 * WIDE + 128
    return jnp.concatenate([got[128:129, :], got[at : at + 1, :]], axis=1)


def half_of(ref, odd):
    return ref.at[:, pl.ds(pl.multiple_of(odd * W, W), W)]


def second(total_rows, keep, guest, got, new_guest, sums, final, kept, done):
    crosses = from_wide(got, 0)
    grams = from_wide(got, 64)
    rows, cols = square_index()
    on_diagonal = jnp.where(rows == cols, grams, 0.0)
    mean_keep = jnp.sum(on_diagonal, axis=1, keepdims=True) / total_rows
    mean_guest = guest_squares(got) / total_rows
    sign = jnp.where(lax.rem(lax.axis_index("col"), 2) == 1, -0.5, 0.5) / total_rows
    x = crosses * (sign * lax.rsqrt(mean_keep + 1e-06)) * lax.rsqrt(mean_guest + 1e-06)
    flipped_x = split(x.T)
    x = split(x)
    s_guest = product(flipped_x, flipped_x, 1, 1)
    s_keep = product(x, x, 1, 1)
    old_keep, old_guest = keep[...], guest[...]
    mixed_keep = old_keep - product(split(old_guest), x, 1, 1)
    mixed_guest = old_guest + product(split(old_keep), x)
    z_guest, z = roots(s_guest, s_keep)
    zs, zs_guest = split(z), split(z_guest)
    kept[...] = product(split(mixed_keep), zs)
    odd = lax.rem(lax.axis_index("col"), 2)
    copy = pltpu.make_async_copy(kept, half_of(final, odd), done)
    copy.start()
    new_guest[...] = product(split(mixed_guest), zs_guest)
    cross = split(crosses)
    flipped = grams.T
    of_keep = split(jnp.where(rows <= cols, grams, flipped))
    of_guest = jnp.where(rows > cols, grams, flipped)
    of_guest = split(jnp.where(rows == cols, guest_squares(got), of_guest))
    v = product(flipped_x, zs)
    w = product(x, zs_guest)
    vs, ws = split(v), split(w)
    sum_keep = jnp.sum(
        z * (product(of_keep, zs) - 2.0 * product(cross, vs)) + v * product(of_guest, vs),
        axis=0,
        keepdims=True,
    )
    sum_guest = jnp.sum(
        z_guest * product(of_guest, zs_guest)
        + w * (product(of_keep, ws) + 2.0 * product(cross, zs_guest)),
        axis=0,
        keepdims=True,
    )
    four = [sum_keep[:, :128], sum_keep[:, 128:], sum_guest[:, :128], sum_guest[:, 128:]]
    tile = jnp.maximum(jnp.concatenate(four + four, axis=0) / total_rows, 0.0)
    for r in range(4 * N_COL // 8):
        sums[8 * r : 8 * r + 8, :] = tile
    copy.wait()


def finish(hits, back, table, begun, final, means, picked, done):
    del begun
    col = lax.axis_index("col")
    copy = pltpu.make_async_copy(back, half_of(final, 1 - lax.rem(col, 2)), done.at[0])
    copy.start()
    for k in range(2):
        one = jnp.zeros((2, 128), jnp.float32)
        for c in range(N_COL):
            kept = table[4 * c : 4 * c + 2, :]
            at = 4 * ((c + (2 if c % 2 else -2)) % N_COL) + 2
            hosted = table[at : at + 2, :]
            for b, part in enumerate((hosted, kept) if c % 2 else (kept, hosted)):
                seat = 2 * N_COL * k + 2 * c + b
                one += jnp.where(hits[seat : seat + 1, :] > 0.5, part, 0.0)
        picked[2 * k : 2 * k + 2, :] = one
    means_copy = pltpu.make_async_copy(picked, means, done.at[1])
    means_copy.start()
    copy.wait()
    means_copy.wait()


VMEM = pl.BlockSpec(memory_space=pltpu.VMEM)
SMEM = pl.BlockSpec(memory_space=pltpu.SMEM)
HBM = pl.BlockSpec(memory_space=pltpu.HBM)


def local(body, flops, *shapes, ins=None, outs=None, scratch=(), aliases=None, limit=LIMIT):
    out = [jax.ShapeDtypeStruct(shape, jnp.float32) for shape in shapes]
    outs = outs or [VMEM] * len(out)
    one = len(out) == 1

    def call(*args):
        moved = sum(4 * a.size for a in args) + sum(4 * s.size for s in out)
        return pl.pallas_call(
            body,
            out_shape=out[0] if one else out,
            in_specs=ins or [VMEM] * len(args),
            out_specs=outs[0] if one else outs,
            scratch_shapes=scratch,
            input_output_aliases=aliases or {},
            cost_estimate=pl.CostEstimate(flops=flops, bytes_accessed=moved, transcendentals=0),
            compiler_params=pltpu.CompilerParams(vmem_limit_bytes=limit),
        )(*args)

    return call


def swapped(block):
    return lax.ppermute(
        block, "col", [(c, (c + (2 if c % 2 else -2)) % N_COL) for c in range(N_COL)]
    )


def swapped_back(block):
    return lax.ppermute(
        block, "col", [(c, (c + (-2 if c % 2 else 2)) % N_COL) for c in range(N_COL)]
    )


ROW = ("z", "far", "near", "x")


def exchange(pieces, axis):
    n = lax.axis_size(axis)
    rows = pieces.shape[0] // n
    shape = (n, rows, 128) if rows % 4 == 0 else (n, 1, rows * 128)
    split_up = pieces.reshape(shape)
    return lax.all_to_all(split_up, axis, 0, 0, tiled=True).reshape(pieces.shape)


def on_device(matrix, seats):
    total_rows = matrix.shape[0] * N_ROW
    one = 6 * W**3
    sent = local(
        pack_first,
        one,
        (NARROW * EIGHT, 128),
        ins=[HBM],
        limit=LOAD_LIMIT,
        scratch=[pltpu.VMEM((W, 2 * W), jnp.float32), pltpu.SemaphoreType.DMA((LOADS,))],
    )(matrix)
    folded = local(functools.partial(fold, NARROW), 1, (NARROW * EIGHT, 128))(
        exchange(sent, ("z", "x"))
    )
    tiles = local(functools.partial(fold_first, total_rows), 1, (64 * EIGHT, 128))(
        exchange(folded, ("far", "near"))
    )
    tiles = exchange(tiles, ("z", "x"))
    move = local(first_move, 5 * one, (W, W))(matrix, tiles)
    guest = swapped(move)
    keep, gram, hits = local(
        first_keep, 6 * one, (W, W), (W, W), (4 * N_COL, 128), ins=[VMEM, VMEM, SMEM]
    )(matrix, tiles, seats)
    sent = local(pack_second, 2 * one, (WIDE * EIGHT, 128))(keep, guest, gram)
    fold_eight = local(functools.partial(fold, WIDE), 1, (WIDE * EIGHT, 128))
    folded = fold_eight(exchange(sent, ("near", "x")))
    folded = fold_eight(exchange(folded, ("z", "far")))
    got = exchange(folded, ("near", "x"))
    new_guest, means, begun = local(
        functools.partial(second, total_rows),
        18 * one,
        (W, W),
        (4 * N_COL, 128),
        (W, 2 * W),
        outs=[VMEM, VMEM, HBM],
        scratch=[pltpu.VMEM((W, W), jnp.float32), pltpu.SemaphoreType.DMA],
    )(keep, guest, got)
    back = swapped_back(new_guest)
    table = exchange(means, "col")
    final, picked = local(
        finish,
        1,
        (W, 2 * W),
        (4, 128),
        ins=[VMEM, VMEM, VMEM, HBM],
        outs=[HBM, HBM],
        scratch=[pltpu.VMEM((4, 128), jnp.float32), pltpu.SemaphoreType.DMA((2,))],
        aliases={3: 0},
    )(hits, back, table, begun)
    return (final, picked.reshape(2 * W))


def solution(mesh):
    parts = Mesh(mesh.devices.reshape(N_COL, *ROW_PARTS), ("col",) + ROW)
    placed = (P(ROW, "col"), P())
    return jax.shard_map(
        on_device,
        mesh=parts,
        in_specs=placed,
        out_specs=(P(ROW, "col"), P("col")),
        check_vma=False,
    )
```

```python
import functools

import jax
import jax.numpy as jnp
from jax import lax
from jax.experimental import pallas as pl
from jax.experimental.pallas import tpu as pltpu
from jax.sharding import Mesh
from jax.sharding import PartitionSpec as P

W = 256
N_ROW = 64
N_COL = 8
ZL, Y, X = 2, 8, 4
EIGHT = 8
NARROW = 66
WIDE = 136
LOADS = 8
LIMIT = 32 * 1024 * 1024
LOAD_LIMIT = 56000000


def split(a):
    high = a.astype(jnp.bfloat16)
    return high, (a - high.astype(jnp.float32)).astype(jnp.bfloat16)


def product(a, b, ca=1, cb=0):
    def one(p, q):
        return lax.dot_general(
            p, q, (((ca,), (cb,)), ((), ())), preferred_element_type=jnp.float32
        )

    return one(a[0], b[0]) + (one(a[0], b[1]) + one(a[1], b[0]))


def root(s, also):
    parts = split(s)
    s2 = product(parts, parts)
    other = also()
    rows = lax.broadcasted_iota(jnp.int32, s.shape, 0)
    cols = lax.broadcasted_iota(jnp.int32, s.shape, 1)
    eye = jnp.where(rows == cols, 1.0, 0.0).astype(jnp.float32)
    base = eye - 0.5 * s + 0.375 * s2
    return base + product(split(s2), split(0.0625 * s2 - 0.3125 * s)), other


def unstacked(ref):
    return jnp.concatenate([ref[:W, :], ref[W:, :]], axis=1)


def roots(*squares):
    parts = [split(s) for s in squares]
    seconds = [product(p, p) for p in parts]
    rows, cols = square_index()
    eye = jnp.where(rows == cols, 1.0, 0.0).astype(jnp.float32)
    return [
        eye - 0.5 * s + 0.375 * s2 + product(split(s2), split(0.0625 * s2 - 0.3125 * s))
        for s, s2 in zip(squares, seconds)
    ]


def column_squares(block):
    return jnp.sum(block * block, axis=0, keepdims=True)


def halves(matrix):
    odd = lax.rem(lax.axis_index("col"), 2)
    keep = matrix[:, pl.ds(pl.multiple_of(odd * W, W), W)]
    move = matrix[:, pl.ds(pl.multiple_of((1 - odd) * W, W), W)]
    return keep, move


def pack_first(whole, out, matrix, arrived):
    rows = W // LOADS
    copies = [
        pltpu.make_async_copy(
            whole.at[pl.ds(k * rows, rows)], matrix.at[pl.ds(k * rows, rows)], arrived.at[k]
        )
        for k in range(LOADS)
    ]
    for copy in copies:
        copy.start()
    for copy in copies:
        copy.wait()
    keep, move = halves(matrix)
    cross = stacked(product(split(keep), split(move), 0, 0))
    norm_keep, norm_move = column_squares(keep), column_squares(move)
    for r in range(EIGHT):
        at = NARROW * r
        out[at : at + 64, :] = cross[64 * r : 64 * r + 64]
        half = (r % 4) // 2
        out[at + 64 : at + 65, :] = norm_keep[:, 128 * half : 128 * half + 128]
        out[at + 65 : at + 66, :] = norm_move[:, 128 * (r // 4) : 128 * (r // 4) + 128]


def square_index():
    rows = lax.broadcasted_iota(jnp.int32, (W, W), 0)
    return rows, lax.broadcasted_iota(jnp.int32, (W, W), 1)


def stacked(block):
    return jnp.concatenate([block[:, :128], block[:, 128:]], axis=0)


def pack_second(keep, guest, gram_keep, out):
    parts = split(guest[...])
    cross = stacked(product(split(keep[...]), parts, 0, 0))
    rows, cols = square_index()
    grams = stacked(jnp.where(rows <= cols, gram_keep[...], product(parts, parts, 0, 0)))
    norms = column_squares(guest[...])
    norms = jnp.concatenate([norms[:, :128], norms[:, 128:]] * 4, axis=0)
    for r in range(EIGHT):
        at = WIDE * r
        out[at : at + 64, :] = cross[64 * r : 64 * r + 64]
        out[at + 64 : at + 128, :] = grams[64 * r : 64 * r + 64]
        out[at + 128 : at + 136, :] = norms


def added(got, size):
    piece = got[0:size, :]
    for r in range(1, EIGHT):
        piece += got[size * r : size * r + size, :]
    return piece


def fold(size, got, out):
    piece = added(got, size)
    for r in range(EIGHT):
        out[size * r : size * r + size, :] = piece


def fold_first(total_rows, got, out):
    piece = added(got, NARROW) / total_rows
    sign = jnp.where(lax.rem(lax.axis_index("col"), 2) == 1, -0.5, 0.5)
    first = 64 * lax.rem(lax.axis_index("x"), 2)
    lanes = lax.broadcasted_iota(jnp.int32, (64, 128), 1)
    rows = lax.broadcasted_iota(jnp.int32, (64, 128), 0)
    mean_keep = jnp.sum(
        jnp.where(lanes == first + rows, piece[64:65], 0.0), axis=1, keepdims=True
    )
    x = sign * piece[:64] / jnp.sqrt((mean_keep + 1e-06) * (piece[65:66] + 1e-06))
    for r in range(EIGHT):
        out[64 * r : 64 * r + 64, :] = x


def from_wide(ref, first):
    at = [WIDE * r + first for r in range(EIGHT)]
    left = [ref[k : k + 64, :] for k in at[:4]]
    right = [ref[k : k + 64, :] for k in at[4:]]
    return jnp.concatenate(
        [jnp.concatenate(left, axis=0), jnp.concatenate(right, axis=0)], axis=1
    )


def first_move(matrix, tiles, out):
    keep, move = halves(matrix)
    x = split(unstacked(tiles))
    z, mixed = root(product(x, x, 0, 0), lambda: move + product(split(keep), x))
    out[...] = product(split(mixed), split(z))


def first_keep(matrix, tiles, seats, out, gram, hits):
    first = 2 * lax.axis_index("col")
    for k in range(2):
        for seat in range(2 * N_COL):
            at = 2 * N_COL * k + seat
            hit = jnp.where(seats[seat] == first + k, 1.0, 0.0).astype(jnp.float32)
            hits[at : at + 1, :] = jnp.full((1, 128), hit)
    keep, move = halves(matrix)
    x = split(unstacked(tiles))
    z, mixed = root(product(x, x, 1, 1), lambda: keep - product(split(move), x, 1, 1))
    kept = product(split(mixed), split(z))
    out[...] = kept
    parts = split(kept)
    gram[...] = product(parts, parts, 0, 0)


def guest_squares(got):
    return jnp.concatenate([got[128:129, :], got[129:130, :]], axis=1)


def half_of(ref, odd):
    return ref.at[:, pl.ds(pl.multiple_of(odd * W, W), W)]


def second(total_rows, keep, guest, got, new_guest, sums, final, kept, done):
    crosses = from_wide(got, 0)
    grams = from_wide(got, 64)
    rows, cols = square_index()
    on_diagonal = jnp.where(rows == cols, grams, 0.0)
    mean_keep = jnp.sum(on_diagonal, axis=1, keepdims=True) / total_rows
    mean_guest = guest_squares(got) / total_rows
    sign = jnp.where(lax.rem(lax.axis_index("col"), 2) == 1, -0.5, 0.5) / total_rows
    x = crosses * (sign * lax.rsqrt(mean_keep + 1e-06)) * lax.rsqrt(mean_guest + 1e-06)
    flipped_x = split(x.T)
    x = split(x)
    s_guest = product(flipped_x, flipped_x, 1, 1)
    s_keep = product(x, x, 1, 1)
    old_keep, old_guest = keep[...], guest[...]
    mixed_keep = old_keep - product(split(old_guest), x, 1, 1)
    mixed_guest = old_guest + product(split(old_keep), x)
    z_guest, z = roots(s_guest, s_keep)
    zs, zs_guest = split(z), split(z_guest)
    kept[...] = product(split(mixed_keep), zs)
    odd = lax.rem(lax.axis_index("col"), 2)
    copy = pltpu.make_async_copy(kept, half_of(final, odd), done)
    copy.start()
    new_guest[...] = product(split(mixed_guest), zs_guest)
    cross = split(crosses)
    flipped = grams.T
    of_keep = split(jnp.where(rows <= cols, grams, flipped))
    of_guest = jnp.where(rows > cols, grams, flipped)
    of_guest = split(jnp.where(rows == cols, guest_squares(got), of_guest))
    v = product(flipped_x, zs)
    w = product(x, zs_guest)
    vs, ws = split(v), split(w)
    sum_keep = jnp.sum(
        z * (product(of_keep, zs) - 2.0 * product(cross, vs)) + v * product(of_guest, vs),
        axis=0,
        keepdims=True,
    )
    sum_guest = jnp.sum(
        z_guest * product(of_guest, zs_guest)
        + w * (product(of_keep, ws) + 2.0 * product(cross, zs_guest)),
        axis=0,
        keepdims=True,
    )
    four = [sum_keep[:, :128], sum_keep[:, 128:], sum_guest[:, :128], sum_guest[:, 128:]]
    tile = jnp.maximum(jnp.concatenate(four + four, axis=0) / total_rows, 0.0)
    for r in range(4 * N_COL // 8):
        sums[8 * r : 8 * r + 8, :] = tile
    copy.wait()


def finish(hits, back, table, begun, final, means, picked, done):
    del begun
    col = lax.axis_index("col")
    copy = pltpu.make_async_copy(back, half_of(final, 1 - lax.rem(col, 2)), done.at[0])
    copy.start()
    for k in range(2):
        one = jnp.zeros((2, 128), jnp.float32)
        for c in range(N_COL):
            kept = table[4 * c : 4 * c + 2, :]
            at = 4 * ((c + (2 if c % 2 else -2)) % N_COL) + 2
            hosted = table[at : at + 2, :]
            for b, part in enumerate((hosted, kept) if c % 2 else (kept, hosted)):
                seat = 2 * N_COL * k + 2 * c + b
                one += jnp.where(hits[seat : seat + 1, :] > 0.5, part, 0.0)
        picked[2 * k : 2 * k + 2, :] = one
    means_copy = pltpu.make_async_copy(picked, means, done.at[1])
    means_copy.start()
    copy.wait()
    means_copy.wait()


VMEM = pl.BlockSpec(memory_space=pltpu.VMEM)
SMEM = pl.BlockSpec(memory_space=pltpu.SMEM)
HBM = pl.BlockSpec(memory_space=pltpu.HBM)


def local(body, flops, *shapes, ins=None, outs=None, scratch=(), aliases=None, limit=LIMIT):
    out = [jax.ShapeDtypeStruct(shape, jnp.float32) for shape in shapes]
    outs = outs or [VMEM] * len(out)
    one = len(out) == 1

    def call(*args):
        moved = sum(4 * a.size for a in args) + sum(4 * s.size for s in out)
        return pl.pallas_call(
            body,
            out_shape=out[0] if one else out,
            in_specs=ins or [VMEM] * len(args),
            out_specs=outs[0] if one else outs,
            scratch_shapes=scratch,
            input_output_aliases=aliases or {},
            cost_estimate=pl.CostEstimate(flops=flops, bytes_accessed=moved, transcendentals=0),
            compiler_params=pltpu.CompilerParams(vmem_limit_bytes=limit),
        )(*args)

    return call


def swapped(block):
    return lax.ppermute(
        block, "col", [(c, (c + (2 if c % 2 else -2)) % N_COL) for c in range(N_COL)]
    )


def swapped_back(block):
    return lax.ppermute(
        block, "col", [(c, (c + (-2 if c % 2 else 2)) % N_COL) for c in range(N_COL)]
    )


ROW = ("zl", "y", "x")


def exchange(pieces, axis):
    n = lax.axis_size(axis)
    rows = pieces.shape[0] // n
    shape = (n, rows, 128) if rows % 4 == 0 else (n, 1, rows * 128)
    split_up = pieces.reshape(shape)
    return lax.all_to_all(split_up, axis, 0, 0, tiled=True).reshape(pieces.shape)


def on_device(matrix, seats):
    total_rows = matrix.shape[0] * N_ROW
    one = 6 * W**3
    sent = local(
        pack_first,
        one,
        (NARROW * EIGHT, 128),
        ins=[HBM],
        limit=LOAD_LIMIT,
        scratch=[pltpu.VMEM((W, 2 * W), jnp.float32), pltpu.SemaphoreType.DMA((LOADS,))],
    )(matrix)
    folded = local(functools.partial(fold, NARROW), 1, (NARROW * EIGHT, 128))(
        exchange(sent, ("zl", "x"))
    )
    tiles = local(functools.partial(fold_first, total_rows), 1, (64 * EIGHT, 128))(
        exchange(folded, "y")
    )
    tiles = exchange(tiles, ("zl", "x"))
    move = local(first_move, 5 * one, (W, W))(matrix, tiles)
    guest = swapped(move)
    keep, gram, hits = local(
        first_keep, 6 * one, (W, W), (W, W), (4 * N_COL, 128), ins=[VMEM, VMEM, SMEM]
    )(matrix, tiles, seats)
    sent = local(pack_second, 2 * one, (WIDE * EIGHT, 128))(keep, guest, gram)
    fold_eight = local(functools.partial(fold, WIDE), 1, (WIDE * EIGHT, 128))
    folded = fold_eight(exchange(sent, ("zl", "x")))
    folded = fold_eight(exchange(folded, "y"))
    got = exchange(folded, ("zl", "x"))
    new_guest, means, begun = local(
        functools.partial(second, total_rows),
        18 * one,
        (W, W),
        (4 * N_COL, 128),
        (W, 2 * W),
        outs=[VMEM, VMEM, HBM],
        scratch=[pltpu.VMEM((W, W), jnp.float32), pltpu.SemaphoreType.DMA],
    )(keep, guest, got)
    back = swapped_back(new_guest)
    table = exchange(means, "col")
    final, picked = local(
        finish,
        1,
        (W, 2 * W),
        (4, 128),
        ins=[VMEM, VMEM, VMEM, HBM],
        outs=[HBM, HBM],
        scratch=[pltpu.VMEM((4, 128), jnp.float32), pltpu.SemaphoreType.DMA((2,))],
        aliases={3: 0},
    )(hits, back, table, begun)
    return (final, picked.reshape(2 * W))


def solution(mesh):
    parts = Mesh(mesh.devices.reshape(N_COL, ZL, Y, X), ("col",) + ROW)
    placed = (P(ROW, "col"), P())
    return jax.shard_map(
        on_device,
        mesh=parts,
        in_specs=placed,
        out_specs=(P(ROW, "col"), P("col")),
        check_vma=False,
    )
```

```python
import functools

import jax
import jax.numpy as jnp
from jax import lax
from jax.experimental import pallas as pl
from jax.experimental.pallas import tpu as pltpu
from jax.sharding import Mesh
from jax.sharding import PartitionSpec as P

W = 256
N_ROW = 64
N_COL = 8
ZL, Y, X = 2, 8, 4
EIGHT = 8
NARROW = 72
WIDE = 136
LOADS = 8
LIMIT = 32 * 1024 * 1024
LOAD_LIMIT = 56000000


def split(a):
    high = a.astype(jnp.bfloat16)
    return high, (a - high.astype(jnp.float32)).astype(jnp.bfloat16)


def product(a, b, ca=1, cb=0):
    def one(p, q):
        return lax.dot_general(
            p, q, (((ca,), (cb,)), ((), ())), preferred_element_type=jnp.float32
        )

    return one(a[0], b[0]) + (one(a[0], b[1]) + one(a[1], b[0]))


def root(s, also):
    parts = split(s)
    s2 = product(parts, parts)
    other = also()
    rows = lax.broadcasted_iota(jnp.int32, s.shape, 0)
    cols = lax.broadcasted_iota(jnp.int32, s.shape, 1)
    eye = jnp.where(rows == cols, 1.0, 0.0).astype(jnp.float32)
    base = eye - 0.5 * s + 0.375 * s2
    return base + product(split(s2), split(0.0625 * s2 - 0.3125 * s)), other


def unstacked(ref):
    return jnp.concatenate([ref[:W, :], ref[W:, :]], axis=1)


def roots(*squares):
    parts = [split(s) for s in squares]
    seconds = [product(p, p) for p in parts]
    rows, cols = square_index()
    eye = jnp.where(rows == cols, 1.0, 0.0).astype(jnp.float32)
    return [
        eye - 0.5 * s + 0.375 * s2 + product(split(s2), split(0.0625 * s2 - 0.3125 * s))
        for s, s2 in zip(squares, seconds)
    ]


def column_squares(block):
    return jnp.sum(block * block, axis=0, keepdims=True)


def halves(matrix):
    odd = lax.rem(lax.axis_index("col"), 2)
    keep = matrix[:, pl.ds(pl.multiple_of(odd * W, W), W)]
    move = matrix[:, pl.ds(pl.multiple_of((1 - odd) * W, W), W)]
    return keep, move


def pack_first(whole, out, matrix, arrived):
    rows = W // LOADS
    copies = [
        pltpu.make_async_copy(
            whole.at[pl.ds(k * rows, rows)], matrix.at[pl.ds(k * rows, rows)], arrived.at[k]
        )
        for k in range(LOADS)
    ]
    for copy in copies:
        copy.start()
    for copy in copies:
        copy.wait()
    keep, move = halves(matrix)
    cross = stacked(product(split(keep), split(move), 0, 0))
    norm_keep, norm_move = column_squares(keep), column_squares(move)
    for r in range(EIGHT):
        at = NARROW * r
        out[at : at + 64, :] = cross[64 * r : 64 * r + 64]
        half = (r % 4) // 2
        pair = [norm_keep[:, 128 * half : 128 * half + 128]]
        pair.append(norm_move[:, 128 * (r // 4) : 128 * (r // 4) + 128])
        out[at + 64 : at + 72, :] = jnp.concatenate(pair * 4, axis=0)


def square_index():
    rows = lax.broadcasted_iota(jnp.int32, (W, W), 0)
    return rows, lax.broadcasted_iota(jnp.int32, (W, W), 1)


def stacked(block):
    return jnp.concatenate([block[:, :128], block[:, 128:]], axis=0)


def pack_second(keep, guest, gram_keep, out):
    parts = split(guest[...])
    cross = stacked(product(split(keep[...]), parts, 0, 0))
    rows, cols = square_index()
    grams = stacked(jnp.where(rows <= cols, gram_keep[...], product(parts, parts, 0, 0)))
    norms = column_squares(guest[...])
    norms = jnp.concatenate([norms[:, :128], norms[:, 128:]] * 4, axis=0)
    for r in range(EIGHT):
        at = WIDE * r
        out[at : at + 64, :] = cross[64 * r : 64 * r + 64]
        out[at + 64 : at + 128, :] = grams[64 * r : 64 * r + 64]
        out[at + 128 : at + 136, :] = norms


def added(got, size):
    piece = got[0:size, :]
    for r in range(1, EIGHT):
        piece += got[size * r : size * r + size, :]
    return piece


def fold(size, got, out):
    piece = added(got, size)
    for r in range(EIGHT):
        out[size * r : size * r + size, :] = piece


def fold_first(total_rows, got, out):
    piece = added(got, NARROW) / total_rows
    sign = jnp.where(lax.rem(lax.axis_index("col"), 2) == 1, -0.5, 0.5)
    first = 64 * lax.rem(lax.axis_index("x"), 2)
    lanes = lax.broadcasted_iota(jnp.int32, (64, 128), 1)
    rows = lax.broadcasted_iota(jnp.int32, (64, 128), 0)
    mean_keep = jnp.sum(
        jnp.where(lanes == first + rows, piece[64:65], 0.0), axis=1, keepdims=True
    )
    x = sign * piece[:64] / jnp.sqrt((mean_keep + 1e-06) * (piece[65:66] + 1e-06))
    for r in range(EIGHT):
        out[64 * r : 64 * r + 64, :] = x


def from_wide(ref, first):
    at = [WIDE * r + first for r in range(EIGHT)]
    left = [ref[k : k + 64, :] for k in at[:4]]
    right = [ref[k : k + 64, :] for k in at[4:]]
    return jnp.concatenate(
        [jnp.concatenate(left, axis=0), jnp.concatenate(right, axis=0)], axis=1
    )


def first_move(matrix, tiles, out):
    keep, move = halves(matrix)
    x = split(unstacked(tiles))
    z, mixed = root(product(x, x, 0, 0), lambda: move + product(split(keep), x))
    out[...] = product(split(mixed), split(z))


def first_keep(matrix, tiles, seats, out, gram, hits):
    first = 2 * lax.axis_index("col")
    for k in range(2):
        for seat in range(2 * N_COL):
            at = 2 * N_COL * k + seat
            hit = jnp.where(seats[seat] == first + k, 1.0, 0.0).astype(jnp.float32)
            hits[at : at + 1, :] = jnp.full((1, 128), hit)
    keep, move = halves(matrix)
    x = split(unstacked(tiles))
    z, mixed = root(product(x, x, 1, 1), lambda: keep - product(split(move), x, 1, 1))
    kept = product(split(mixed), split(z))
    out[...] = kept
    parts = split(kept)
    gram[...] = product(parts, parts, 0, 0)


def guest_squares(got):
    return jnp.concatenate([got[128:129, :], got[129:130, :]], axis=1)


def half_of(ref, odd):
    return ref.at[:, pl.ds(pl.multiple_of(odd * W, W), W)]


def second(total_rows, keep, guest, got, new_guest, sums, x_out, z_out):
    crosses = from_wide(got, 0)
    grams = from_wide(got, 64)
    rows, cols = square_index()
    on_diagonal = jnp.where(rows == cols, grams, 0.0)
    mean_keep = jnp.sum(on_diagonal, axis=1, keepdims=True) / total_rows
    mean_guest = guest_squares(got) / total_rows
    sign = jnp.where(lax.rem(lax.axis_index("col"), 2) == 1, -0.5, 0.5) / total_rows
    x = crosses * (sign * lax.rsqrt(mean_keep + 1e-06)) * lax.rsqrt(mean_guest + 1e-06)
    x_out[...] = x
    flipped_x = split(x.T)
    x = split(x)
    s_guest = product(flipped_x, flipped_x, 1, 1)
    s_keep = product(x, x, 1, 1)
    mixed_guest = guest[...] + product(split(keep[...]), x)
    z_guest, z = roots(s_guest, s_keep)
    zs, zs_guest = split(z), split(z_guest)
    z_out[...] = z
    new_guest[...] = product(split(mixed_guest), zs_guest)
    cross = split(crosses)
    flipped = grams.T
    of_keep = split(jnp.where(rows <= cols, grams, flipped))
    of_guest = jnp.where(rows > cols, grams, flipped)
    of_guest = split(jnp.where(rows == cols, guest_squares(got), of_guest))
    v = product(flipped_x, zs)
    w = product(x, zs_guest)
    vs, ws = split(v), split(w)
    sum_keep = jnp.sum(
        z * (product(of_keep, zs) - 2.0 * product(cross, vs)) + v * product(of_guest, vs),
        axis=0,
        keepdims=True,
    )
    sum_guest = jnp.sum(
        z_guest * product(of_guest, zs_guest)
        + w * (product(of_keep, ws) + 2.0 * product(cross, zs_guest)),
        axis=0,
        keepdims=True,
    )
    four = [sum_keep[:, :128], sum_keep[:, 128:], sum_guest[:, :128], sum_guest[:, 128:]]
    tile = jnp.maximum(jnp.concatenate(four + four, axis=0) / total_rows, 0.0)
    for r in range(4 * N_COL // 8):
        sums[8 * r : 8 * r + 8, :] = tile


def second_keep(keep, guest, x_in, z_in, final, kept, done):
    mixed = keep[...] - product(split(guest[...]), split(x_in[...]), 1, 1)
    kept[...] = product(split(mixed), split(z_in[...]))
    odd = lax.rem(lax.axis_index("col"), 2)
    copy = pltpu.make_async_copy(kept, half_of(final, odd), done)
    copy.start()
    copy.wait()


def finish(hits, back, table, begun, final, means, picked, done):
    del begun
    col = lax.axis_index("col")
    copy = pltpu.make_async_copy(back, half_of(final, 1 - lax.rem(col, 2)), done.at[0])
    copy.start()
    for k in range(2):
        one = jnp.zeros((2, 128), jnp.float32)
        for c in range(N_COL):
            kept = table[4 * c : 4 * c + 2, :]
            at = 4 * ((c + (2 if c % 2 else -2)) % N_COL) + 2
            hosted = table[at : at + 2, :]
            for b, part in enumerate((hosted, kept) if c % 2 else (kept, hosted)):
                seat = 2 * N_COL * k + 2 * c + b
                one += jnp.where(hits[seat : seat + 1, :] > 0.5, part, 0.0)
        picked[2 * k : 2 * k + 2, :] = one
    means_copy = pltpu.make_async_copy(picked, means, done.at[1])
    means_copy.start()
    copy.wait()
    means_copy.wait()


VMEM = pl.BlockSpec(memory_space=pltpu.VMEM)
SMEM = pl.BlockSpec(memory_space=pltpu.SMEM)
HBM = pl.BlockSpec(memory_space=pltpu.HBM)


def local(body, flops, *shapes, ins=None, outs=None, scratch=(), aliases=None, limit=LIMIT):
    out = [jax.ShapeDtypeStruct(shape, jnp.float32) for shape in shapes]
    outs = outs or [VMEM] * len(out)
    one = len(out) == 1

    def call(*args):
        moved = sum(4 * a.size for a in args) + sum(4 * s.size for s in out)
        return pl.pallas_call(
            body,
            out_shape=out[0] if one else out,
            in_specs=ins or [VMEM] * len(args),
            out_specs=outs[0] if one else outs,
            scratch_shapes=scratch,
            input_output_aliases=aliases or {},
            cost_estimate=pl.CostEstimate(flops=flops, bytes_accessed=moved, transcendentals=0),
            compiler_params=pltpu.CompilerParams(vmem_limit_bytes=limit),
        )(*args)

    return call


def swapped(block):
    return lax.ppermute(
        block, "col", [(c, (c + (2 if c % 2 else -2)) % N_COL) for c in range(N_COL)]
    )


def swapped_back(block):
    return lax.ppermute(
        block, "col", [(c, (c + (-2 if c % 2 else 2)) % N_COL) for c in range(N_COL)]
    )


ROW = ("zl", "y", "x")


def exchange(pieces, axis):
    split_up = pieces.reshape(lax.axis_size(axis), -1, 128)
    return lax.all_to_all(split_up, axis, 0, 0, tiled=True).reshape(pieces.shape)


def on_device(matrix, seats):
    total_rows = matrix.shape[0] * N_ROW
    one = 6 * W**3
    sent = local(
        pack_first,
        one,
        (NARROW * EIGHT, 128),
        ins=[HBM],
        limit=LOAD_LIMIT,
        scratch=[pltpu.VMEM((W, 2 * W), jnp.float32), pltpu.SemaphoreType.DMA((LOADS,))],
    )(matrix)
    folded = local(functools.partial(fold, NARROW), 1, (NARROW * EIGHT, 128))(
        exchange(sent, ("zl", "x"))
    )
    tiles = local(functools.partial(fold_first, total_rows), 1, (64 * EIGHT, 128))(
        exchange(folded, "y")
    )
    tiles = exchange(tiles, ("zl", "x"))
    move = local(first_move, 5 * one, (W, W))(matrix, tiles)
    guest = swapped(move)
    keep, gram, hits = local(
        first_keep, 6 * one, (W, W), (W, W), (4 * N_COL, 128), ins=[VMEM, VMEM, SMEM]
    )(matrix, tiles, seats)
    sent = local(pack_second, 2 * one, (WIDE * EIGHT, 128))(keep, guest, gram)
    fold_eight = local(functools.partial(fold, WIDE), 1, (WIDE * EIGHT, 128))
    folded = fold_eight(exchange(sent, ("zl", "x")))
    folded = fold_eight(exchange(folded, "y"))
    got = exchange(folded, ("zl", "x"))
    new_guest, means, x, z = local(
        functools.partial(second, total_rows),
        16 * one,
        (W, W),
        (4 * N_COL, 128),
        (W, W),
        (W, W),
    )(keep, guest, got)
    begun = local(
        second_keep,
        2 * one,
        (W, 2 * W),
        outs=[HBM],
        scratch=[pltpu.VMEM((W, W), jnp.float32), pltpu.SemaphoreType.DMA],
    )(keep, guest, x, z)
    back = swapped_back(new_guest)
    table = exchange(means, "col")
    final, picked = local(
        finish,
        1,
        (W, 2 * W),
        (4, 128),
        ins=[VMEM, VMEM, VMEM, HBM],
        outs=[HBM, HBM],
        scratch=[pltpu.VMEM((4, 128), jnp.float32), pltpu.SemaphoreType.DMA((2,))],
        aliases={3: 0},
    )(hits, back, table, begun)
    return (final, picked.reshape(2 * W))


def solution(mesh):
    parts = Mesh(mesh.devices.reshape(N_COL, ZL, Y, X), ("col",) + ROW)
    placed = (P(ROW, "col"), P())
    return jax.shard_map(
        on_device,
        mesh=parts,
        in_specs=placed,
        out_specs=(P(ROW, "col"), P("col")),
        check_vma=False,
    )
```

```python
import functools

import jax
import jax.numpy as jnp
from jax import lax
from jax.experimental import pallas as pl
from jax.experimental.pallas import tpu as pltpu
from jax.sharding import Mesh
from jax.sharding import PartitionSpec as P

W = 256
N_ROW = 64
N_COL = 8
ZL, Y, X = 2, 8, 4
EIGHT = 8
NARROW = 72
WIDE = 136
LOADS = 8
LIMIT = 32 * 1024 * 1024
LOAD_LIMIT = 56000000


def split(a):
    high = a.astype(jnp.bfloat16)
    return high, (a - high.astype(jnp.float32)).astype(jnp.bfloat16)


def product(a, b, ca=1, cb=0):
    def one(p, q):
        return lax.dot_general(
            p, q, (((ca,), (cb,)), ((), ())), preferred_element_type=jnp.float32
        )

    return one(a[0], b[0]) + (one(a[0], b[1]) + one(a[1], b[0]))


def root(s, also):
    parts = split(s)
    s2 = product(parts, parts)
    other = also()
    rows = lax.broadcasted_iota(jnp.int32, s.shape, 0)
    cols = lax.broadcasted_iota(jnp.int32, s.shape, 1)
    eye = jnp.where(rows == cols, 1.0, 0.0).astype(jnp.float32)
    base = eye - 0.5 * s + 0.375 * s2
    return base + product(split(s2), split(0.0625 * s2 - 0.3125 * s)), other


def unstacked(ref):
    return jnp.concatenate([ref[:W, :], ref[W:, :]], axis=1)


def roots(*squares):
    parts = [split(s) for s in squares]
    seconds = [product(p, p) for p in parts]
    rows, cols = square_index()
    eye = jnp.where(rows == cols, 1.0, 0.0).astype(jnp.float32)
    return [
        eye - 0.5 * s + 0.375 * s2 + product(split(s2), split(0.0625 * s2 - 0.3125 * s))
        for s, s2 in zip(squares, seconds)
    ]


def column_squares(block):
    return jnp.sum(block * block, axis=0, keepdims=True)


def halves(matrix):
    odd = lax.rem(lax.axis_index("col"), 2)
    keep = matrix[:, pl.ds(pl.multiple_of(odd * W, W), W)]
    move = matrix[:, pl.ds(pl.multiple_of((1 - odd) * W, W), W)]
    return keep, move


def pack_first(whole, out, matrix, arrived):
    rows = W // LOADS
    copies = [
        pltpu.make_async_copy(
            whole.at[pl.ds(k * rows, rows)], matrix.at[pl.ds(k * rows, rows)], arrived.at[k]
        )
        for k in range(LOADS)
    ]
    for copy in copies:
        copy.start()
    for copy in copies:
        copy.wait()
    keep, move = halves(matrix)
    cross = stacked(product(split(keep), split(move), 0, 0))
    norm_keep, norm_move = column_squares(keep), column_squares(move)
    for r in range(EIGHT):
        at = NARROW * r
        out[at : at + 64, :] = cross[64 * r : 64 * r + 64]
        half = (r % 4) // 2
        pair = [norm_keep[:, 128 * half : 128 * half + 128]]
        pair.append(norm_move[:, 128 * (r // 4) : 128 * (r // 4) + 128])
        out[at + 64 : at + 72, :] = jnp.concatenate(pair * 4, axis=0)


def square_index():
    rows = lax.broadcasted_iota(jnp.int32, (W, W), 0)
    return rows, lax.broadcasted_iota(jnp.int32, (W, W), 1)


def stacked(block):
    return jnp.concatenate([block[:, :128], block[:, 128:]], axis=0)


def pack_second(keep, guest, gram_keep, out):
    parts = split(guest[...])
    cross = stacked(product(split(keep[...]), parts, 0, 0))
    rows, cols = square_index()
    grams = stacked(jnp.where(rows <= cols, gram_keep[...], product(parts, parts, 0, 0)))
    norms = column_squares(guest[...])
    norms = jnp.concatenate([norms[:, :128], norms[:, 128:]] * 4, axis=0)
    for r in range(EIGHT):
        at = WIDE * r
        out[at : at + 64, :] = cross[64 * r : 64 * r + 64]
        out[at + 64 : at + 128, :] = grams[64 * r : 64 * r + 64]
        out[at + 128 : at + 136, :] = norms


def added(got, size):
    piece = got[0:size, :]
    for r in range(1, EIGHT):
        piece += got[size * r : size * r + size, :]
    return piece


def fold(size, got, out):
    piece = added(got, size)
    for r in range(EIGHT):
        out[size * r : size * r + size, :] = piece


def fold_first(total_rows, got, out):
    piece = added(got, NARROW) / total_rows
    sign = jnp.where(lax.rem(lax.axis_index("col"), 2) == 1, -0.5, 0.5)
    first = 64 * lax.rem(lax.axis_index("x"), 2)
    lanes = lax.broadcasted_iota(jnp.int32, (64, 128), 1)
    rows = lax.broadcasted_iota(jnp.int32, (64, 128), 0)
    mean_keep = jnp.sum(
        jnp.where(lanes == first + rows, piece[64:65], 0.0), axis=1, keepdims=True
    )
    x = sign * piece[:64] / jnp.sqrt((mean_keep + 1e-06) * (piece[65:66] + 1e-06))
    for r in range(EIGHT):
        out[64 * r : 64 * r + 64, :] = x


def from_wide(ref, first):
    at = [WIDE * r + first for r in range(EIGHT)]
    left = [ref[k : k + 64, :] for k in at[:4]]
    right = [ref[k : k + 64, :] for k in at[4:]]
    return jnp.concatenate(
        [jnp.concatenate(left, axis=0), jnp.concatenate(right, axis=0)], axis=1
    )


def first_move(matrix, tiles, out):
    keep, move = halves(matrix)
    x = split(unstacked(tiles))
    z, mixed = root(product(x, x, 0, 0), lambda: move + product(split(keep), x))
    out[...] = product(split(mixed), split(z))


def first_keep(matrix, tiles, seats, out, gram, hits):
    first = 2 * lax.axis_index("col")
    for k in range(2):
        for seat in range(2 * N_COL):
            at = 2 * N_COL * k + seat
            hit = jnp.where(seats[seat] == first + k, 1.0, 0.0).astype(jnp.float32)
            hits[at : at + 1, :] = jnp.full((1, 128), hit)
    keep, move = halves(matrix)
    x = split(unstacked(tiles))
    z, mixed = root(product(x, x, 1, 1), lambda: keep - product(split(move), x, 1, 1))
    kept = product(split(mixed), split(z))
    out[...] = kept
    parts = split(kept)
    gram[...] = product(parts, parts, 0, 0)


def guest_squares(got):
    return jnp.concatenate([got[128:129, :], got[129:130, :]], axis=1)


def half_of(ref, odd):
    return ref.at[:, pl.ds(pl.multiple_of(odd * W, W), W)]


def second(total_rows, keep, guest, got, new_guest, sums_out, x_out, z_out, sums, done):
    crosses = from_wide(got, 0)
    grams = from_wide(got, 64)
    rows, cols = square_index()
    on_diagonal = jnp.where(rows == cols, grams, 0.0)
    mean_keep = jnp.sum(on_diagonal, axis=1, keepdims=True) / total_rows
    mean_guest = guest_squares(got) / total_rows
    sign = jnp.where(lax.rem(lax.axis_index("col"), 2) == 1, -0.5, 0.5) / total_rows
    x = crosses * (sign * lax.rsqrt(mean_keep + 1e-06)) * lax.rsqrt(mean_guest + 1e-06)
    x_out[...] = x
    flipped_x = split(x.T)
    x = split(x)
    s_guest = product(flipped_x, flipped_x, 1, 1)
    s_keep = product(x, x, 1, 1)
    mixed_guest = guest[...] + product(split(keep[...]), x)
    z_guest, z = roots(s_guest, s_keep)
    zs, zs_guest = split(z), split(z_guest)
    z_out[...] = z
    cross = split(crosses)
    flipped = grams.T
    of_keep = split(jnp.where(rows <= cols, grams, flipped))
    of_guest = jnp.where(rows > cols, grams, flipped)
    of_guest = split(jnp.where(rows == cols, guest_squares(got), of_guest))
    v = product(flipped_x, zs)
    w = product(x, zs_guest)
    vs, ws = split(v), split(w)
    sum_keep = jnp.sum(
        z * (product(of_keep, zs) - 2.0 * product(cross, vs)) + v * product(of_guest, vs),
        axis=0,
        keepdims=True,
    )
    sum_guest = jnp.sum(
        z_guest * product(of_guest, zs_guest)
        + w * (product(of_keep, ws) + 2.0 * product(cross, zs_guest)),
        axis=0,
        keepdims=True,
    )
    four = [sum_keep[:, :128], sum_keep[:, 128:], sum_guest[:, :128], sum_guest[:, 128:]]
    tile = jnp.maximum(jnp.concatenate(four + four, axis=0) / total_rows, 0.0)
    for r in range(4 * N_COL // 8):
        sums[8 * r : 8 * r + 8, :] = tile
    copy = pltpu.make_async_copy(sums, sums_out, done)
    copy.start()
    new_guest[...] = product(split(mixed_guest), zs_guest)
    copy.wait()


def second_keep(keep, guest, x_in, z_in, final, kept, done):
    mixed = keep[...] - product(split(guest[...]), split(x_in[...]), 1, 1)
    kept[...] = product(split(mixed), split(z_in[...]))
    odd = lax.rem(lax.axis_index("col"), 2)
    copy = pltpu.make_async_copy(kept, half_of(final, odd), done)
    copy.start()
    copy.wait()


def finish(hits, back, table, begun, final, means, picked, done):
    del begun
    col = lax.axis_index("col")
    copy = pltpu.make_async_copy(back, half_of(final, 1 - lax.rem(col, 2)), done.at[0])
    copy.start()
    for k in range(2):
        one = jnp.zeros((2, 128), jnp.float32)
        for c in range(N_COL):
            kept = table[4 * c : 4 * c + 2, :]
            at = 4 * ((c + (2 if c % 2 else -2)) % N_COL) + 2
            hosted = table[at : at + 2, :]
            for b, part in enumerate((hosted, kept) if c % 2 else (kept, hosted)):
                seat = 2 * N_COL * k + 2 * c + b
                one += jnp.where(hits[seat : seat + 1, :] > 0.5, part, 0.0)
        picked[2 * k : 2 * k + 2, :] = one
    means_copy = pltpu.make_async_copy(picked, means, done.at[1])
    means_copy.start()
    copy.wait()
    means_copy.wait()


VMEM = pl.BlockSpec(memory_space=pltpu.VMEM)
SMEM = pl.BlockSpec(memory_space=pltpu.SMEM)
HBM = pl.BlockSpec(memory_space=pltpu.HBM)


def local(body, flops, *shapes, ins=None, outs=None, scratch=(), aliases=None, limit=LIMIT):
    out = [jax.ShapeDtypeStruct(shape, jnp.float32) for shape in shapes]
    outs = outs or [VMEM] * len(out)
    one = len(out) == 1

    def call(*args):
        moved = sum(4 * a.size for a in args) + sum(4 * s.size for s in out)
        return pl.pallas_call(
            body,
            out_shape=out[0] if one else out,
            in_specs=ins or [VMEM] * len(args),
            out_specs=outs[0] if one else outs,
            scratch_shapes=scratch,
            input_output_aliases=aliases or {},
            cost_estimate=pl.CostEstimate(flops=flops, bytes_accessed=moved, transcendentals=0),
            compiler_params=pltpu.CompilerParams(vmem_limit_bytes=limit),
        )(*args)

    return call


def swapped(block):
    return lax.ppermute(
        block, "col", [(c, (c + (2 if c % 2 else -2)) % N_COL) for c in range(N_COL)]
    )


def swapped_back(block):
    return lax.ppermute(
        block, "col", [(c, (c + (-2 if c % 2 else 2)) % N_COL) for c in range(N_COL)]
    )


ROW = ("zl", "y", "x")


def exchange(pieces, axis):
    split_up = pieces.reshape(lax.axis_size(axis), -1, 128)
    return lax.all_to_all(split_up, axis, 0, 0, tiled=True).reshape(pieces.shape)


def on_device(matrix, seats):
    total_rows = matrix.shape[0] * N_ROW
    one = 6 * W**3
    sent = local(
        pack_first,
        one,
        (NARROW * EIGHT, 128),
        ins=[HBM],
        limit=LOAD_LIMIT,
        scratch=[pltpu.VMEM((W, 2 * W), jnp.float32), pltpu.SemaphoreType.DMA((LOADS,))],
    )(matrix)
    folded = local(functools.partial(fold, NARROW), 1, (NARROW * EIGHT, 128))(
        exchange(sent, ("zl", "x"))
    )
    tiles = local(functools.partial(fold_first, total_rows), 1, (64 * EIGHT, 128))(
        exchange(folded, "y")
    )
    tiles = exchange(tiles, ("zl", "x"))
    move = local(first_move, 5 * one, (W, W))(matrix, tiles)
    guest = swapped(move)
    keep, gram, hits = local(
        first_keep, 6 * one, (W, W), (W, W), (4 * N_COL, 128), ins=[VMEM, VMEM, SMEM]
    )(matrix, tiles, seats)
    sent = local(pack_second, 2 * one, (WIDE * EIGHT, 128))(keep, guest, gram)
    fold_eight = local(functools.partial(fold, WIDE), 1, (WIDE * EIGHT, 128))
    folded = fold_eight(exchange(sent, ("zl", "x")))
    folded = fold_eight(exchange(folded, "y"))
    got = exchange(folded, ("zl", "x"))
    new_guest, means, x, z = local(
        functools.partial(second, total_rows),
        16 * one,
        (W, W),
        (4 * N_COL, 128),
        (W, W),
        (W, W),
        outs=[VMEM, HBM, VMEM, VMEM],
        scratch=[pltpu.VMEM((4 * N_COL, 128), jnp.float32), pltpu.SemaphoreType.DMA],
    )(keep, guest, got)
    begun = local(
        second_keep,
        2 * one,
        (W, 2 * W),
        outs=[HBM],
        scratch=[pltpu.VMEM((W, W), jnp.float32), pltpu.SemaphoreType.DMA],
    )(keep, guest, x, z)
    back = swapped_back(new_guest)
    table = exchange(means, "col")
    final, picked = local(
        finish,
        1,
        (W, 2 * W),
        (4, 128),
        ins=[VMEM, VMEM, VMEM, HBM],
        outs=[HBM, HBM],
        scratch=[pltpu.VMEM((4, 128), jnp.float32), pltpu.SemaphoreType.DMA((2,))],
        aliases={3: 0},
    )(hits, back, table, begun)
    return (final, picked.reshape(2 * W))


def solution(mesh):
    parts = Mesh(mesh.devices.reshape(N_COL, ZL, Y, X), ("col",) + ROW)
    placed = (P(ROW, "col"), P())
    return jax.shard_map(
        on_device,
        mesh=parts,
        in_specs=placed,
        out_specs=(P(ROW, "col"), P("col")),
        check_vma=False,
    )
```

```python
import functools

import jax
import jax.numpy as jnp
from jax import lax
from jax.experimental import pallas as pl
from jax.experimental.pallas import tpu as pltpu
from jax.sharding import Mesh
from jax.sharding import PartitionSpec as P

W = 256
N_ROW = 64
N_COL = 8
ZL, Y, X = 2, 8, 4
EIGHT = 8
NARROW = 66
WIDE = 129
LOADS = 8
LIMIT = 32 * 1024 * 1024
LOAD_LIMIT = 56000000


def split(a):
    high = a.astype(jnp.bfloat16)
    return high, (a - high.astype(jnp.float32)).astype(jnp.bfloat16)


def product(a, b, ca=1, cb=0):
    def one(p, q):
        return lax.dot_general(
            p, q, (((ca,), (cb,)), ((), ())), preferred_element_type=jnp.float32
        )

    return one(a[0], b[0]) + (one(a[0], b[1]) + one(a[1], b[0]))


def root(s, also):
    parts = split(s)
    s2 = product(parts, parts)
    other = also()
    rows = lax.broadcasted_iota(jnp.int32, s.shape, 0)
    cols = lax.broadcasted_iota(jnp.int32, s.shape, 1)
    eye = jnp.where(rows == cols, 1.0, 0.0).astype(jnp.float32)
    base = eye - 0.5 * s + 0.375 * s2
    return base + product(split(s2), split(0.0625 * s2 - 0.3125 * s)), other


def unstacked(ref):
    return jnp.concatenate([ref[:W, :], ref[W:, :]], axis=1)


def roots(*squares):
    parts = [split(s) for s in squares]
    seconds = [product(p, p) for p in parts]
    rows, cols = square_index()
    eye = jnp.where(rows == cols, 1.0, 0.0).astype(jnp.float32)
    return [
        eye - 0.5 * s + 0.375 * s2 + product(split(s2), split(0.0625 * s2 - 0.3125 * s))
        for s, s2 in zip(squares, seconds)
    ]


def column_squares(block):
    return jnp.sum(block * block, axis=0, keepdims=True)


def halves(matrix):
    odd = lax.rem(lax.axis_index("col"), 2)
    keep = matrix[:, pl.ds(pl.multiple_of(odd * W, W), W)]
    move = matrix[:, pl.ds(pl.multiple_of((1 - odd) * W, W), W)]
    return keep, move


def pack_first(whole, out, matrix, arrived):
    rows = W // LOADS
    copies = [
        pltpu.make_async_copy(
            whole.at[pl.ds(k * rows, rows)], matrix.at[pl.ds(k * rows, rows)], arrived.at[k]
        )
        for k in range(LOADS)
    ]
    for copy in copies:
        copy.start()
    for copy in copies:
        copy.wait()
    keep, move = halves(matrix)
    cross = stacked(product(split(keep), split(move), 0, 0))
    norm_keep, norm_move = column_squares(keep), column_squares(move)
    for r in range(EIGHT):
        at = NARROW * r
        out[at : at + 64, :] = cross[64 * r : 64 * r + 64]
        half = (r % 4) // 2
        out[at + 64 : at + 65, :] = norm_keep[:, 128 * half : 128 * half + 128]
        out[at + 65 : at + 66, :] = norm_move[:, 128 * (r // 4) : 128 * (r // 4) + 128]


def square_index():
    rows = lax.broadcasted_iota(jnp.int32, (W, W), 0)
    return rows, lax.broadcasted_iota(jnp.int32, (W, W), 1)


def stacked(block):
    return jnp.concatenate([block[:, :128], block[:, 128:]], axis=0)


def pack_second(keep, guest, gram_keep, out):
    parts = split(guest[...])
    cross = stacked(product(split(keep[...]), parts, 0, 0))
    rows, cols = square_index()
    grams = stacked(jnp.where(rows <= cols, gram_keep[...], product(parts, parts, 0, 0)))
    norms = column_squares(guest[...])
    for r in range(EIGHT):
        at = WIDE * r
        out[at : at + 64, :] = cross[64 * r : 64 * r + 64]
        out[at + 64 : at + 128, :] = grams[64 * r : 64 * r + 64]
        out[at + 128 : at + 129, :] = norms[:, 128 * (r // 4) : 128 * (r // 4) + 128]


def added(got, size):
    piece = got[0:size, :]
    for r in range(1, EIGHT):
        piece += got[size * r : size * r + size, :]
    return piece


def fold(size, got, out):
    piece = added(got, size)
    for r in range(EIGHT):
        out[size * r : size * r + size, :] = piece


def fold_first(total_rows, got, out):
    piece = added(got, NARROW) / total_rows
    sign = jnp.where(lax.rem(lax.axis_index("col"), 2) == 1, -0.5, 0.5)
    first = 64 * lax.rem(lax.axis_index("x"), 2)
    lanes = lax.broadcasted_iota(jnp.int32, (64, 128), 1)
    rows = lax.broadcasted_iota(jnp.int32, (64, 128), 0)
    mean_keep = jnp.sum(
        jnp.where(lanes == first + rows, piece[64:65], 0.0), axis=1, keepdims=True
    )
    x = sign * piece[:64] / jnp.sqrt((mean_keep + 1e-06) * (piece[65:66] + 1e-06))
    for r in range(EIGHT):
        out[64 * r : 64 * r + 64, :] = x


def from_wide(ref, first):
    at = [WIDE * r + first for r in range(EIGHT)]
    left = [ref[k : k + 64, :] for k in at[:4]]
    right = [ref[k : k + 64, :] for k in at[4:]]
    return jnp.concatenate(
        [jnp.concatenate(left, axis=0), jnp.concatenate(right, axis=0)], axis=1
    )


def first_move(matrix, tiles, out):
    keep, move = halves(matrix)
    x = split(unstacked(tiles))
    z, mixed = root(product(x, x, 0, 0), lambda: move + product(split(keep), x))
    out[...] = product(split(mixed), split(z))


def first_keep(matrix, tiles, seats, out, gram, hits):
    first = 2 * lax.axis_index("col")
    for k in range(2):
        for seat in range(2 * N_COL):
            at = 2 * N_COL * k + seat
            hit = jnp.where(seats[seat] == first + k, 1.0, 0.0).astype(jnp.float32)
            hits[at : at + 1, :] = jnp.full((1, 128), hit)
    keep, move = halves(matrix)
    x = split(unstacked(tiles))
    z, mixed = root(product(x, x, 1, 1), lambda: keep - product(split(move), x, 1, 1))
    kept = product(split(mixed), split(z))
    out[...] = kept
    parts = split(kept)
    gram[...] = product(parts, parts, 0, 0)


def guest_squares(got):
    at = 4 * WIDE + 128
    return jnp.concatenate([got[128:129, :], got[at : at + 1, :]], axis=1)


def half_of(ref, odd):
    return ref.at[:, pl.ds(pl.multiple_of(odd * W, W), W)]


def second(total_rows, keep, guest, got, new_guest, sums, x_out, z_out):
    crosses = from_wide(got, 0)
    grams = from_wide(got, 64)
    rows, cols = square_index()
    on_diagonal = jnp.where(rows == cols, grams, 0.0)
    mean_keep = jnp.sum(on_diagonal, axis=1, keepdims=True) / total_rows
    mean_guest = guest_squares(got) / total_rows
    sign = jnp.where(lax.rem(lax.axis_index("col"), 2) == 1, -0.5, 0.5) / total_rows
    x = crosses * (sign * lax.rsqrt(mean_keep + 1e-06)) * lax.rsqrt(mean_guest + 1e-06)
    x_out[...] = x
    flipped_x = split(x.T)
    x = split(x)
    s_guest = product(flipped_x, flipped_x, 1, 1)
    s_keep = product(x, x, 1, 1)
    mixed_guest = guest[...] + product(split(keep[...]), x)
    z_guest, z = roots(s_guest, s_keep)
    zs, zs_guest = split(z), split(z_guest)
    z_out[...] = z
    new_guest[...] = product(split(mixed_guest), zs_guest)
    cross = split(crosses)
    flipped = grams.T
    of_keep = split(jnp.where(rows <= cols, grams, flipped))
    of_guest = jnp.where(rows > cols, grams, flipped)
    of_guest = split(jnp.where(rows == cols, guest_squares(got), of_guest))
    v = product(flipped_x, zs)
    w = product(x, zs_guest)
    vs, ws = split(v), split(w)
    sum_keep = jnp.sum(
        z * (product(of_keep, zs) - 2.0 * product(cross, vs)) + v * product(of_guest, vs),
        axis=0,
        keepdims=True,
    )
    sum_guest = jnp.sum(
        z_guest * product(of_guest, zs_guest)
        + w * (product(of_keep, ws) + 2.0 * product(cross, zs_guest)),
        axis=0,
        keepdims=True,
    )
    four = [sum_keep[:, :128], sum_keep[:, 128:], sum_guest[:, :128], sum_guest[:, 128:]]
    tile = jnp.maximum(jnp.concatenate(four + four, axis=0) / total_rows, 0.0)
    for r in range(4 * N_COL // 8):
        sums[8 * r : 8 * r + 8, :] = tile


def second_keep(keep, guest, x_in, z_in, final, kept, done):
    mixed = keep[...] - product(split(guest[...]), split(x_in[...]), 1, 1)
    kept[...] = product(split(mixed), split(z_in[...]))
    odd = lax.rem(lax.axis_index("col"), 2)
    copy = pltpu.make_async_copy(kept, half_of(final, odd), done)
    copy.start()
    copy.wait()


def finish(hits, back, table, begun, final, means, picked, done):
    del begun
    col = lax.axis_index("col")
    copy = pltpu.make_async_copy(back, half_of(final, 1 - lax.rem(col, 2)), done.at[0])
    copy.start()
    for k in range(2):
        one = jnp.zeros((2, 128), jnp.float32)
        for c in range(N_COL):
            kept = table[4 * c : 4 * c + 2, :]
            at = 4 * ((c + (2 if c % 2 else -2)) % N_COL) + 2
            hosted = table[at : at + 2, :]
            for b, part in enumerate((hosted, kept) if c % 2 else (kept, hosted)):
                seat = 2 * N_COL * k + 2 * c + b
                one += jnp.where(hits[seat : seat + 1, :] > 0.5, part, 0.0)
        picked[2 * k : 2 * k + 2, :] = one
    means_copy = pltpu.make_async_copy(picked, means, done.at[1])
    means_copy.start()
    copy.wait()
    means_copy.wait()


VMEM = pl.BlockSpec(memory_space=pltpu.VMEM)
SMEM = pl.BlockSpec(memory_space=pltpu.SMEM)
HBM = pl.BlockSpec(memory_space=pltpu.HBM)


def local(body, flops, *shapes, ins=None, outs=None, scratch=(), aliases=None, limit=LIMIT):
    out = [jax.ShapeDtypeStruct(shape, jnp.float32) for shape in shapes]
    outs = outs or [VMEM] * len(out)
    one = len(out) == 1

    def call(*args):
        moved = sum(4 * a.size for a in args) + sum(4 * s.size for s in out)
        return pl.pallas_call(
            body,
            out_shape=out[0] if one else out,
            in_specs=ins or [VMEM] * len(args),
            out_specs=outs[0] if one else outs,
            scratch_shapes=scratch,
            input_output_aliases=aliases or {},
            cost_estimate=pl.CostEstimate(flops=flops, bytes_accessed=moved, transcendentals=0),
            compiler_params=pltpu.CompilerParams(vmem_limit_bytes=limit),
        )(*args)

    return call


def swapped(block):
    return lax.ppermute(
        block, "col", [(c, (c + (2 if c % 2 else -2)) % N_COL) for c in range(N_COL)]
    )


def swapped_back(block):
    return lax.ppermute(
        block, "col", [(c, (c + (-2 if c % 2 else 2)) % N_COL) for c in range(N_COL)]
    )


ROW = ("zl", "y", "x")


def exchange(pieces, axis):
    n = lax.axis_size(axis)
    rows = pieces.shape[0] // n
    shape = (n, rows, 128) if rows % 4 == 0 else (n, 1, rows * 128)
    split_up = pieces.reshape(shape)
    return lax.all_to_all(split_up, axis, 0, 0, tiled=True).reshape(pieces.shape)


def on_device(matrix, seats):
    total_rows = matrix.shape[0] * N_ROW
    one = 6 * W**3
    sent = local(
        pack_first,
        one,
        (NARROW * EIGHT, 128),
        ins=[HBM],
        limit=LOAD_LIMIT,
        scratch=[pltpu.VMEM((W, 2 * W), jnp.float32), pltpu.SemaphoreType.DMA((LOADS,))],
    )(matrix)
    folded = local(functools.partial(fold, NARROW), 1, (NARROW * EIGHT, 128))(
        exchange(sent, ("zl", "x"))
    )
    tiles = local(functools.partial(fold_first, total_rows), 1, (64 * EIGHT, 128))(
        exchange(folded, "y")
    )
    tiles = exchange(tiles, ("zl", "x"))
    move = local(first_move, 5 * one, (W, W))(matrix, tiles)
    guest = swapped(move)
    keep, gram, hits = local(
        first_keep, 6 * one, (W, W), (W, W), (4 * N_COL, 128), ins=[VMEM, VMEM, SMEM]
    )(matrix, tiles, seats)
    sent = local(pack_second, 2 * one, (WIDE * EIGHT, 128))(keep, guest, gram)
    fold_eight = local(functools.partial(fold, WIDE), 1, (WIDE * EIGHT, 128))
    folded = fold_eight(exchange(sent, ("zl", "x")))
    folded = fold_eight(exchange(folded, "y"))
    got = exchange(folded, ("zl", "x"))
    new_guest, means, x, z = local(
        functools.partial(second, total_rows),
        16 * one,
        (W, W),
        (4 * N_COL, 128),
        (W, W),
        (W, W),
    )(keep, guest, got)
    begun = local(
        second_keep,
        2 * one,
        (W, 2 * W),
        outs=[HBM],
        scratch=[pltpu.VMEM((W, W), jnp.float32), pltpu.SemaphoreType.DMA],
    )(keep, guest, x, z)
    back = swapped_back(new_guest)
    table = exchange(means, "col")
    final, picked = local(
        finish,
        1,
        (W, 2 * W),
        (4, 128),
        ins=[VMEM, VMEM, VMEM, HBM],
        outs=[HBM, HBM],
        scratch=[pltpu.VMEM((4, 128), jnp.float32), pltpu.SemaphoreType.DMA((2,))],
        aliases={3: 0},
    )(hits, back, table, begun)
    return (final, picked.reshape(2 * W))


def solution(mesh):
    parts = Mesh(mesh.devices.reshape(N_COL, ZL, Y, X), ("col",) + ROW)
    placed = (P(ROW, "col"), P())
    return jax.shard_map(
        on_device,
        mesh=parts,
        in_specs=placed,
        out_specs=(P(ROW, "col"), P("col")),
        check_vma=False,
    )
```
